32 devices in a mesh: seq: 8 (over z, x), wa: 4 (over y, core).
Axes of the slice: x: 2, y: 2, z: 4, core: 2. Of those that a mesh axis runs over, the one named last changes fastest.
Arguments:
- inputs: float32 [12288, 1024], P('seq'), may hold values from -6 to 6
- seq_starts: int32 [12288], P('seq'), may hold values from 0 to 1, as said below
- ln_gain: float32 [1024], replicated, may hold values from 0.5 to 1.5
- ln_bias: float32 [1024], replicated, may hold values from -1.8 to 1.8
- w_gate: float32 [1024, 3072], P(None, 'wa'), may hold values from -0.1875 to 0.1875
- b_gate: float32 [3072], P('wa'), may hold values from -1.8 to 1.8
- w_reduce: float32 [1024, 512], P(None, 'wa'), may hold values from -0.1875 to 0.1875
- b_reduce: float32 [512], P('wa'), may hold values from -1.8 to 1.8
- ssm_rate: float32 [512], P('wa'), may hold values from 2e-05 to 0.02
- ssm_step: float32 [512], P('wa'), may hold values from 0.5 to 2
- ssm_out: float32 [512], P('wa'), may hold values from 0.3 to 3
- w_expand: float32 [512, 3072], P(None, 'wa'), may hold values from -0.5 to 0.5
- b_expand: float32 [3072], P('wa'), may hold values from -1.8 to 1.8
- w_down: float32 [1024, 3072], P(None, 'wa'), may hold values from -0.4375 to 0.4375
- b_down: float32 [1024], replicated, may hold values from -1.8 to 1.8
- cotangent: float32 [12288, 1024], P('seq', 'wa'), may hold values from -6 to 6
Outputs:
- output: float32 [12288, 1024], P('seq', 'wa')
- grad_inputs: float32 [12288, 1024], P('seq')
- grad_ln_gain: float32 [1024], P('seq')
- grad_ln_bias: float32 [1024], P('seq')
- grad_w_gate: float32 [1024, 3072], P('seq', 'wa')
- grad_b_gate: float32 [3072], P(('wa', 'seq'))
- grad_w_reduce: float32 [1024, 512], P('seq', 'wa')
- grad_b_reduce: float32 [512], P(('wa', 'seq'))
- grad_ssm_rate: float32 [512], P(('wa', 'seq'))
- grad_ssm_step: float32 [512], P(('wa', 'seq'))
- grad_ssm_out: float32 [512], P(('wa', 'seq'))
- grad_w_expand: float32 [512, 3072], P('seq', 'wa')
- grad_b_expand: float32 [3072], P(('wa', 'seq'))
- grad_w_down: float32 [1024, 3072], P('seq', 'wa')
- grad_b_down: float32 [1024], P('seq')
The draws below stay inside these ranges and needn't reach their ends.
Inputs may be any that keep to these rules, and one draw needn't show every extreme that they name: `seq_starts`: token 0 is a start; the sequences that the starts delimit hold 1024 to 4096 tokens, except the last, which may be shorter, and one holds exactly 4096.
All inputs are finite; a program needn't handle non-finite values.
Results may differ from the reference program's by a relative error of at most 0.0004.
Values sent between devices are 32-bit elements; how exact they have to be, the bound alone decides.
No kernel may reach another device: no remote copies, remote signals or barrier semaphores. Data moves between devices by JAX's collectives and lax.ppermute only.
A program may use at most 128 MiB of HBM per device.

```python
import math
import jax
import jax.numpy as jnp
from jax import lax

D = 1024
F = 3072
H = 512
SEQ_MAX = 4096
SEQ_MIN = 1024
TOKENS = 12288


def draw_seq_starts(key, part):
    count = TOKENS // SEQ_MIN + 1
    lengths = jax.random.randint(jax.random.fold_in(key, 11), (count,), SEQ_MIN, SEQ_MAX + 1)
    slot = jax.random.randint(jax.random.fold_in(key, 12), (), 0, max(1, (TOKENS - SEQ_MAX) // (4 * SEQ_MAX) + 1))
    lengths = jnp.where(jnp.arange(count) == slot, SEQ_MAX, lengths).astype(jnp.int32)
    finishes = jnp.cumsum(lengths).astype(jnp.int32)
    heads = jnp.concatenate([jnp.zeros((1,), jnp.int32), finishes[:-1]]).astype(jnp.int32)
    return jnp.zeros((TOKENS,), jnp.int32).at[heads].set(1, mode='drop')


def raised(result, rng, source, target, blocks, factor):
    owner, partner = [(jnp.arange(result.shape[dim]) // (result.shape[dim] // blocks)).reshape([-1 if axis == dim else 1 for axis in range(result.ndim)]) for dim in (source, target)]
    chosen = jax.random.permutation(rng, blocks)[partner]
    strong = (owner == chosen) | (owner == (partner + blocks // 2) % blocks)
    return jnp.where(strong, factor * result, result)


def block_scale(own_key, extent, pieces, least, largest):
    def one(axis_at, parts):
        steps = jax.random.uniform(jax.random.fold_in(jax.random.fold_in(own_key, 6), axis_at), (parts,), jnp.float32, least / len(pieces), largest / len(pieces))
        return jnp.repeat(jnp.exp(steps), extent[axis_at] // parts).reshape((-1,) + (1,) * (len(extent) - axis_at - 1))

    factor_of = one(*pieces[0])
    for cut in pieces[1:]:
        factor_of = factor_of * one(*cut)
    return factor_of


def normal_values(key, shape, deviation, reach, split=(), kind=jnp.bfloat16):
    loudness = block_scale(key, shape, split, -0.22, 0.18) if split else 1.0
    result = jax.random.normal(key, shape, jnp.float32) * deviation * loudness
    return jnp.minimum(jnp.maximum(result, -reach), reach).astype(kind)


def gaussian_with(own_key, extent, deviation, most, cuts, heavy, dtype=jnp.bfloat16):
    drawn = deviation * jax.random.normal(own_key, extent, jnp.float32)
    if cuts:
        drawn = drawn * block_scale(own_key, extent, cuts, -0.22, 0.18)
    return jnp.clip(raised(drawn, jax.random.fold_in(own_key, 3), *heavy), -most, most).astype(dtype)


def setup_inputs(seed: int = 0) -> dict:
    keys = jax.random.split(jax.random.key(seed), 17)
    inputs = normal_values(keys[0], (TOKENS, D), 1.0, 6.0, ((0, 8),), jnp.float32)
    seq_starts = draw_seq_starts(jax.random.fold_in(keys[16], 71), 0)
    ln_gain = jnp.clip(1.0 + 0.1 * jax.random.normal(keys[2], (D,), jnp.float32), 0.5, 1.5)
    ln_bias = normal_values(keys[3], (D,), 0.3, 1.8, (), jnp.float32)
    w_gate = normal_values(keys[4], (D, F), D ** -0.5, 0.1875, ((1, 4),), jnp.float32)
    b_gate = normal_values(keys[5], (F,), 0.3, 1.8, ((0, 4),), jnp.float32)
    w_reduce = normal_values(keys[6], (D, H), D ** -0.5, 0.1875, ((1, 4),), jnp.float32)
    b_reduce = normal_values(keys[7], (H,), 0.3, 1.8, ((0, 4),), jnp.float32)
    ssm_rate = jnp.clip(jnp.exp(math.log(0.02) - 6.9077553 * jax.random.uniform(keys[8], (H,), jnp.float32) ** block_scale(keys[8], (H,), ((0, 4),), -0.2, 0.2)), 1.9999999494757503e-05, 0.02)
    ssm_step = jnp.clip(jnp.exp(math.log(2.0) - 1.3862944 * jax.random.uniform(keys[9], (H,), jnp.float32) ** block_scale(keys[9], (H,), ((0, 4),), -0.2, 0.2)), 0.5, 2.0)
    ssm_out = jnp.clip(jnp.exp(math.log(3.0) - 2.3025851 * jax.random.uniform(keys[10], (H,), jnp.float32) ** block_scale(keys[10], (H,), ((0, 4),), -0.2, 0.2)), 0.3, 3.0)
    w_expand = normal_values(keys[11], (H, F), (H // 4) ** -0.5, 0.5, ((1, 4),), jnp.float32)
    b_expand = normal_values(keys[12], (F,), 0.3, 1.8, ((0, 4),), jnp.float32)
    w_down = normal_values(keys[13], (D, F), (F // 16) ** -0.5, 0.4375, ((1, 4),), jnp.float32)
    b_down = normal_values(keys[14], (D,), 0.3, 1.8, (), jnp.float32)
    cotangent = gaussian_with(keys[15], (TOKENS, D), 1.0, 6.0, ((0, 8), (1, 4)), (0, 1, 8, 2.0), jnp.float32)
    return dict(inputs=inputs, seq_starts=seq_starts, ln_gain=ln_gain, ln_bias=ln_bias, w_gate=w_gate, b_gate=b_gate, w_reduce=w_reduce, b_reduce=b_reduce, ssm_rate=ssm_rate, ssm_step=ssm_step, ssm_out=ssm_out, w_expand=w_expand, b_expand=b_expand, w_down=w_down, b_down=b_down, cotangent=cotangent)


@jax.custom_vjp
def low(v):
    return lax.optimization_barrier(v.astype(jnp.bfloat16)).astype(jnp.float32)

@jax.custom_vjp
def low_back(v):
    return v

def low_keep(v):
    return (low(v), None)

def low_pass(kept, grad):
    return (grad,)

def back_keep(v):
    return (v, None)

def back_low(kept, grad):
    return (low(grad),)
low.defvjp(low_keep, low_pass)
low_back.defvjp(back_keep, back_low)
HIGHEST = lax.Precision.HIGHEST
EPSILON = 1e-05

def forward(inputs, ln_gain, ln_bias, w_gate, b_gate, w_reduce, b_reduce, ssm_rate, ssm_step, ssm_out, w_expand, b_expand, w_down, b_down, keep_mask):
    row_mean = lax.optimization_barrier(jnp.mean(inputs, axis=1, keepdims=True))
    centred = inputs - row_mean
    variance = lax.optimization_barrier(jnp.mean(centred * centred, axis=1, keepdims=True))
    normed = centred * lax.rsqrt(variance + EPSILON) * ln_gain + ln_bias
    gate_act = jax.nn.gelu(jnp.dot(normed, w_gate, precision=HIGHEST) + b_gate, approximate=False)
    reduced = jax.nn.gelu(jnp.dot(normed, w_reduce, precision=HIGHEST) + b_reduce, approximate=False)
    keep_rate = jnp.exp(-ssm_rate * ssm_step)

    def advance(carried, pair):
        keep_row, driven = pair
        carried = keep_rate * keep_row * carried + (1.0 - keep_rate) * driven
        return (carried, carried)
    _, states = lax.scan(advance, jnp.zeros_like(keep_rate), (keep_mask, reduced))
    mixed = states * ssm_out
    expand = jnp.dot(mixed, w_expand, precision=HIGHEST) + b_expand
    return inputs + jnp.dot(gate_act * expand, w_down.T, precision=HIGHEST) + b_down

def reference(inputs, seq_starts, ln_gain, ln_bias, w_gate, b_gate, w_reduce, b_reduce, ssm_rate, ssm_step, ssm_out, w_expand, b_expand, w_down, b_down, cotangent):
    keep_mask = 1.0 - seq_starts.astype(jnp.float32)[:, None]

    def wrapped(inputs, ln_gain, ln_bias, w_gate, b_gate, w_reduce, b_reduce, ssm_rate, ssm_step, ssm_out, w_expand, b_expand, w_down, b_down):
        return forward(inputs, ln_gain, ln_bias, w_gate, b_gate, w_reduce, b_reduce, ssm_rate, ssm_step, ssm_out, w_expand, b_expand, w_down, b_down, keep_mask)
    output, backward = jax.vjp(wrapped, inputs, ln_gain, ln_bias, w_gate, b_gate, w_reduce, b_reduce, ssm_rate, ssm_step, ssm_out, w_expand, b_expand, w_down, b_down)
    grads = backward(cotangent)
    return (output, grads[0], grads[1], grads[2], grads[3], grads[4], grads[5], grads[6], grads[7], grads[8], grads[9], grads[10], grads[11], grads[12], grads[13])
```

```python
import functools

import jax
import jax.numpy as jnp
from jax import lax
from jax.experimental import pallas as pl
from jax.experimental.pallas import tpu as pltpu
from jax.sharding import PartitionSpec as P

EPSILON = 1e-05
INV_ROOT_TAU = 0.3989422804014327
SEQ_MAX = 4096
F32 = jnp.float32
BF16 = jnp.bfloat16
VMEM_LIMIT = 26 * 2**20
TILE = 256
COST = 10**5
RATE = 5 * 10**7
FILL = 400
NN = ((1,), (0,))
NT = ((1,), (1,))
TN = ((0,), (0,))


def split(value):
    high = value.astype(BF16)
    return high, (value - high.astype(F32)).astype(BF16)


def dot(left, right, dims):
    return lax.dot_general(left, right, (dims, ((), ())), preferred_element_type=F32)


def dot3(left, right, dims):
    (left_high, left_low), (right_high, right_low) = left, right
    return dot(left_high, right_high, dims) + (
        dot(left_high, right_low, dims) + dot(left_low, right_high, dims)
    )


def gelu_parts(v):
    bell = jnp.exp(-0.5 * v * v)
    span = 1.0 + 0.23164189 * jnp.abs(v)
    t = pl.reciprocal(span, approx=True)
    t = t * (2.0 - span * t)
    tail = 0.5 * (1.061405429 * t - 1.453152027)
    tail = tail * t + 0.5 * 1.421413741
    tail = tail * t - 0.5 * 0.284496736
    tail = tail * t + 0.5 * 0.254829592
    tail = tail * t * bell
    cdf = jnp.where(v < 0.0, tail, 1.0 - tail)
    return v * cdf, cdf + (INV_ROOT_TAU * v) * bell


def standardise(values):
    scale = 1.0 / values.shape[1]
    centred = values - jnp.sum(values, axis=1, keepdims=True) * scale
    variance = jnp.sum(centred * centred, axis=1, keepdims=True) * scale
    inv_std = lax.rsqrt(variance + EPSILON)
    return centred * inv_std, inv_std


def row_sums(value):
    return jnp.sum(value.reshape(value.shape[0] // 8, 8, value.shape[1]), axis=0)


def sublane(shape=(8, 128)):
    return lax.broadcasted_iota(jnp.int32, shape, 0)


def wide(row):
    return jnp.broadcast_to(row, (8, row.shape[1]))


def entering(gots):
    total = gots[0][0:1, :]
    keep = gots[0][1:2, :]
    for got in gots[1:]:
        total = total + keep * got[0:1, :]
        keep = keep * got[1:2, :]
    return total


def first_step():
    return pl.program_id(0) == 0


def last_step():
    return pl.program_id(0) == pl.num_programs(0) - 1


def apart():
    return pl.when(pl.program_id(0) >= 0)


def add_to(ref, value):
    @pl.when(first_step())
    def _():
        ref[...] = jnp.zeros_like(ref)

    ref[...] += value


def split_rows(ids_ref, order, source_ref, high, low):
    width = high.shape[0] // len(order)
    for place, r in enumerate(order):
        at = pl.multiple_of((ids_ref[0] ^ r) * width, width)
        to = slice(place * width, (place + 1) * width)
        high[to, :], low[to, :] = split(source_ref[pl.ds(at, width), :])


def reduce_kernel(
    x_ref, gain_ref, shift_ref, w_ref, b_ref, rate_ref, step_ref, mask_ref,
    high_ref, low_ref, red_ref, slope_ref, local_ref, lead_ref, end_ref,
    w_high, w_low, drive_ref, carry_ref,
):
    log_keep = -rate_ref[...] * step_ref[...]
    keep = wide(jnp.exp(log_keep))
    fresh = 1.0 - jnp.exp(log_keep)

    @pl.when(first_step())
    def _():
        w_high[...], w_low[...] = split(w_ref[...])
        carry_ref[0:8, :] = jnp.zeros((8, 128), F32)
        carry_ref[8:16, :] = jnp.ones((8, 128), F32)

    standard, _ = standardise(x_ref[...])
    parts = split(standard * gain_ref[...] + shift_ref[...])
    high_ref[...], low_ref[...] = parts
    pre = dot3(parts, (w_high[...], w_low[...]), NN) + b_ref[...]
    reduced, slope_ref[...] = gelu_parts(pre)
    red_ref[...] = reduced
    drive_ref[...] = fresh * reduced
    at = sublane()
    powers = [keep, keep * keep]
    powers.append(powers[1] * powers[1])
    ramp = jnp.exp((at + 1).astype(F32) * log_keep)

    def step(j, carry):
        state, decay = carry
        here = pl.ds(pl.multiple_of(j * 8, 8), 8)
        value = drive_ref[here, :]
        mask = mask_ref[here, :]
        for power, hop in zip(powers, (1, 2, 4)):
            inside = at >= hop
            value = value + jnp.where(inside, power * mask, 0.0) * pltpu.roll(value, hop, 0)
            mask = jnp.where(inside, mask * pltpu.roll(mask, hop, 0), mask)
        factor = ramp * mask
        value = value + factor * state
        factor = factor * decay
        local_ref[here, :] = value
        lead_ref[here, :] = factor
        return (wide(value[7:8, :]), wide(factor[7:8, :]))

    start = (carry_ref[0:8, :], carry_ref[8:16, :])
    state, decay = lax.fori_loop(0, x_ref.shape[0] // 8, step, start, unroll=8)
    carry_ref[0:8, :] = state
    carry_ref[8:16, :] = decay
    end_ref[...] = jnp.where(at == 0, state, decay)


def gate_kernel(high_ref, low_ref, w_ref, b_ref, act_ref, slope_ref, w_high, w_low):
    @pl.when(first_step())
    def _():
        w_high[...], w_low[...] = split(w_ref[...])

    pre = dot3((high_ref[...], low_ref[...]), (w_high[...], w_low[...]), NN) + b_ref[...]
    act_ref[...], slope_ref[...] = gelu_parts(pre)


def states_kernel(hops, local_ref, lead_ref, red_ref, mask_ref, out_ref, *rest):
    gots, (mixed_ref, states_ref, turn_ref, last_ref) = rest[:hops], rest[hops:]
    enter = entering(gots)

    @pl.when(first_step())
    def _():
        last_ref[...] = wide(enter)

    states = local_ref[...] + lead_ref[...] * enter
    states_ref[...] = states
    mixed_ref[...] = states * out_ref[...]
    first = sublane(states.shape) == 0
    before = jnp.where(first, last_ref[0:1, :], pltpu.roll(states, 1, 0))
    turn_ref[...] = mask_ref[...] * before - red_ref[...]
    last_ref[...] = wide(states[states.shape[0] - 1 :, :])


def cotangent_kernel(
    ids_ref, c0, c1, c2, c3, wd_ref, act_ref, we_ref,
    high_ref, low_ref, gp_ref, ge_high, ge_low, send_ref, c_sum,
    wd_high, wd_low, we_high, we_low,
):
    width = c0.shape[1]

    @pl.when(first_step())
    def _():
        split_rows(ids_ref, range(4), wd_ref, wd_high, wd_low)
        split_rows(ids_ref, (3, 1), we_ref, we_high, we_low)

    for r, c in enumerate((c0, c1, c2, c3)):
        at = slice(r * width, (r + 1) * width)
        high_ref[:, at], low_ref[:, at] = split(c[...])
        add_to(c_sum.at[:, at], row_sums(c[...]))
    grad_product = dot3((high_ref[...], low_ref[...]), (wd_high[...], wd_low[...]), NN)
    gp_ref[...] = grad_product
    ge_high[...], ge_low[...] = split(grad_product * act_ref[...])

    @apart()
    def _():
        send_ref[...] = dot3((ge_high[...], ge_low[...]), (we_high[...], we_low[...]), NT)


def back_kernel(ids_ref, ge_high, ge_low, we_ref, keep_ref, ge_sum, we_high, we_low):
    @pl.when(first_step())
    def _():
        split_rows(ids_ref, (2, 0), we_ref, we_high, we_low)

    keep_ref[...] = dot3((ge_high[...], ge_low[...]), (we_high[...], we_low[...]), NT)
    add_to(ge_sum, row_sums(ge_high[...].astype(F32) + ge_low[...].astype(F32)))


def expand_kernel(
    ids_ref, m0, m1, m2, m3, we_ref, be_ref, wd_ref, act_ref, slope_ref, gp_ref,
    mix_high, mix_low, prod_high, prod_low, gate_high, gate_low, send_ref, keep_ref, gate_sum,
    we_high, we_low, wd_high, wd_low,
):
    here = ids_ref[0]
    own = m0.shape[1]
    width = send_ref.shape[1]

    @pl.when(first_step())
    def _():
        for r in range(4):
            at = pl.multiple_of((here ^ r) * own, own)
            to = slice(r * own, (r + 1) * own)
            we_high[to, :], we_low[to, :] = split(we_ref[pl.ds(at, own), :])
        for place, r in enumerate((3, 2)):
            at = pl.multiple_of((here ^ r) * width, width)
            to = slice(place * width, (place + 1) * width)
            wd_high[to, :], wd_low[to, :] = split(wd_ref[pl.ds(at, width), :])

    for r, m in enumerate((m0, m1, m2, m3)):
        at = slice(r * own, (r + 1) * own)
        mix_high[:, at], mix_low[:, at] = split(m[...])
    expand = dot3((mix_high[...], mix_low[...]), (we_high[...], we_low[...]), NN) + be_ref[...]
    prod_high[...], prod_low[...] = split(act_ref[...] * expand)
    grad_gate = gp_ref[...] * expand * slope_ref[...]
    gate_high[...], gate_low[...] = split(grad_gate)
    add_to(gate_sum, row_sums(grad_gate))

    @apart()
    def _():
        out = dot3((prod_high[...], prod_low[...]), (wd_high[...], wd_low[...]), NT)
        send_ref[...] = out[:, :width]
        keep_ref[...] = out[:, width:]


def output_kernel(
    ids_ref, high_ref, low_ref, wd_ref, x_ref, b_ref, send_ref, keep_ref, wd_high, wd_low
):
    here = ids_ref[0]
    width = send_ref.shape[1]

    @pl.when(first_step())
    def _():
        for place, r in enumerate((1, 0)):
            at = pl.multiple_of((here ^ r) * width, width)
            to = slice(place * width, (place + 1) * width)
            wd_high[to, :], wd_low[to, :] = split(wd_ref[pl.ds(at, width), :])

    out = dot3((high_ref[...], low_ref[...]), (wd_high[...], wd_low[...]), NT)
    send_ref[...] = out[:, :width]
    keep_ref[...] = out[:, width:] + x_ref[...] + b_ref[...]


def adjoint_kernel(
    keep_ref, recv_ref, far_ref, states_ref, mask_ref, out_ref, rate_ref, step_ref,
    local_ref, tail_ref, end_ref, sum_ref, carry_ref,
):
    own = far_ref.shape[1]
    log_keep = -rate_ref[...] * step_ref[...]
    keep = wide(jnp.exp(log_keep))

    @pl.when(first_step())
    def _():
        carry_ref[0:8, :] = jnp.zeros((8, 128), F32)
        carry_ref[8:16, :] = jnp.ones((8, 128), F32)

    at = sublane()
    powers = [keep, keep * keep]
    powers.append(powers[1] * powers[1])
    ramp = jnp.exp((8 - at).astype(F32) * log_keep)
    out_rate = wide(out_ref[...])
    count = far_ref.shape[0] // 8

    def step(n, carry):
        state, decay, total = carry
        here = pl.ds(pl.multiple_of((count - 1 - n) * 8, 8), 8)
        grad = keep_ref[here, own:] + recv_ref[here, own:] + far_ref[here, :]
        total = total + grad * states_ref[here, :]
        drive = grad * out_rate
        mask = mask_ref[here, :]
        value = keep * mask * drive
        for power, hop in zip(powers, (1, 2, 4)):
            inside = at < 8 - hop
            value = value + jnp.where(inside, power * mask, 0.0) * pltpu.roll(value, 8 - hop, 0)
            mask = jnp.where(inside, mask * pltpu.roll(mask, 8 - hop, 0), mask)
        factor = ramp * mask
        value = value + factor * state
        factor = factor * decay
        local_ref[here, :] = drive + jnp.where(at == 7, state, pltpu.roll(value, 7, 0))
        tail_ref[here, :] = jnp.where(at == 7, decay, pltpu.roll(factor, 7, 0))
        return (wide(value[0:1, :]), wide(factor[0:1, :]), total)

    start = (carry_ref[0:8, :], carry_ref[8:16, :], jnp.zeros((8, 128), F32))
    state, decay, total = lax.fori_loop(0, count, step, start, unroll=8)
    carry_ref[0:8, :] = state
    carry_ref[8:16, :] = decay
    end_ref[...] = jnp.where(at == 0, state, decay)
    add_to(sum_ref, total)


def add_norm_sums(ids_ref, x_ref, parts, standard_ref, sums_ref):
    width = parts[0][1].shape[1]
    standard_ref[...], _ = standardise(x_ref[...])
    for r, part in parts:
        at = pl.ds(pl.multiple_of((ids_ref[0] ^ r) * width, width), width)
        sums_ref[0:8, at] += row_sums(part * standard_ref[:, at])
        sums_ref[8:16, at] += row_sums(part)


def normed_far_kernel(
    hops, ids_ref, local_ref, tail_ref, turn_ref, slope_ref, gate_high, gate_low, x_ref,
    wg_ref, wr_ref, rate_ref, step_ref, *rest,
):
    gots = rest[:hops]
    (red_high, red_low, send_ref, keep_ref, turn_sum, red_sum, norm_sum,
     wg_high, wg_low, wr_high, wr_low, standard_ref) = rest[hops:]
    width = send_ref.shape[1]

    @pl.when(first_step())
    def _():
        split_rows(ids_ref, (3, 2), wg_ref, wg_high, wg_low)
        split_rows(ids_ref, (3, 2), wr_ref, wr_high, wr_low)
        norm_sum[...] = jnp.zeros_like(norm_sum)

    adjoint = local_ref[...] + tail_ref[...] * entering(gots)
    fresh = 1.0 - jnp.exp(-rate_ref[...] * step_ref[...])
    grad = fresh * adjoint * slope_ref[...]
    parts = split(grad)
    red_high[...], red_low[...] = parts
    add_to(turn_sum, row_sums(adjoint * turn_ref[...]))
    add_to(red_sum, row_sums(grad))
    back = dot3((gate_high[...], gate_low[...]), (wg_high[...], wg_low[...]), NT)
    back = back + dot3(parts, (wr_high[...], wr_low[...]), NT)
    send_ref[...] = back[:, :width]
    keep_ref[...] = back[:, width:]
    add_norm_sums(ids_ref, x_ref, [(3, back[:, :width]), (2, back[:, width:])], standard_ref, norm_sum)


def normed_near_kernel(
    ids_ref, red_high, red_low, gate_high, gate_low, x_ref, wg_ref, wr_ref, far_sum,
    send_ref, keep_ref, norm_ref, wg_high, wg_low, wr_high, wr_low, standard_ref, norm_sum,
):
    width = send_ref.shape[1]

    @pl.when(first_step())
    def _():
        split_rows(ids_ref, (1, 0), wg_ref, wg_high, wg_low)
        split_rows(ids_ref, (1, 0), wr_ref, wr_high, wr_low)
        norm_sum[...] = far_sum[...]

    back = dot3((gate_high[...], gate_low[...]), (wg_high[...], wg_low[...]), NT)
    back = back + dot3((red_high[...], red_low[...]), (wr_high[...], wr_low[...]), NT)
    send_ref[...] = back[:, :width]
    keep_ref[...] = back[:, width:]
    add_norm_sums(ids_ref, x_ref, [(1, back[:, :width]), (0, back[:, width:])], standard_ref, norm_sum)

    @pl.when(last_step())
    def _():
        gain = jnp.sum(norm_sum[0:8, :], axis=0, keepdims=True)
        shift = jnp.sum(norm_sum[8:16, :], axis=0, keepdims=True)
        norm_ref[...] = jnp.where(sublane(norm_ref.shape) == 0, gain, shift)


def weight_kernel(relative, ids_ref, left_high, left_low, right_high, right_low, keep_ref, send_ref, acc_ref):
    @pl.when(first_step())
    def _():
        acc_ref[...] = jnp.zeros_like(acc_ref)

    for at in range(0, acc_ref.shape[1], 256):
        to = slice(at, at + 256)
        acc_ref[:, to] += dot3((left_high[...], left_low[...]), (right_high[:, to], right_low[:, to]), TN)
    half, rows, _ = keep_ref.shape
    block = acc_ref.shape[0] // 4

    @pl.when(last_step())
    def _():
        for place in range(2 * half):
            at = ids_ref[2 + place] * rows
            if relative:
                at = ((at // block) ^ ids_ref[0]) * block + at % block
            value = acc_ref[pl.ds(pl.multiple_of(at, 8), rows), :]
            if place < half:
                keep_ref[place] = value
            else:
                send_ref[place - half] = value


def reduce_weight_kernel(
    ids_ref, left_high, left_low, right_high, right_low, vector_ref, keep_ref, send_ref, acc_ref
):
    add_to(acc_ref, dot3((left_high[...], left_low[...]), (right_high[...], right_low[...]), TN))
    half, rows, _ = keep_ref.shape
    rows = rows - 8

    @pl.when(last_step())
    def _():
        for place in range(2 * half):
            block = ids_ref[2 + place]
            to, slot = (keep_ref, place) if place < half else (send_ref, place - half)
            to[slot, :rows] = acc_ref[pl.ds(pl.multiple_of(block * rows, 8), rows), :]
            to[slot, rows:] = vector_ref[pl.ds(pl.multiple_of(block * 8, 8), 8), :]


def pack_kernel(own_ref, core_ref, far_ref, far_core_ref, down_ref, gate_ref, expand_ref, red_ref, turn_ref, out_ref,
                vector_ref, whole_ref, here_ref):
    count = vector_ref.shape[0] // 8
    vector_ref[...] = jnp.zeros_like(vector_ref)
    width = down_ref.shape[1] // 4
    here = lax.axis_index("wa")
    for r in range(4):
        at = pl.multiple_of((here ^ r) * width, width)
        here_ref[2:3, pl.ds(at, width)] = jnp.sum(down_ref[:, r * width : (r + 1) * width], axis=0, keepdims=True)
    norm = (own_ref[...] + core_ref[...]) + (far_ref[...] + far_core_ref[...])
    here_ref[0:2, :] = norm[0:2, :]
    rows = [here_ref[0:1, :], here_ref[1:2, :], here_ref[2:3, :]]
    rows += [jnp.sum(ref[...], axis=0, keepdims=True) for ref in (gate_ref, expand_ref, red_ref, turn_ref, out_ref)]
    for k, row in enumerate(rows):
        whole_ref[k : k + 1, : row.shape[1]] = row
    for k, row in enumerate(rows):
        size = row.shape[1] // count
        for d in range(count):
            vector_ref[d * 8 + k : d * 8 + k + 1, :size] = whole_ref[k : k + 1, d * size : (d + 1) * size]


def final_kernel(ids_ref, x_ref, gain_ref, g0, g1, g2, g3, c0, c1, c2, c3, out_ref, grad_ref, cot_ref):
    width = g0.shape[1]
    for r, (g, c) in enumerate(((g0, c0), (g1, c1), (g2, c2), (g3, c3))):
        at = pl.ds(pl.multiple_of((ids_ref[0] ^ r) * width, width), width)
        grad_ref[:, at] = g[...]
        cot_ref[:, at] = c[...]
    scale = 1.0 / x_ref.shape[1]
    standard, inv_std = standardise(x_ref[...])
    scaled = grad_ref[...] * gain_ref[...]
    first = jnp.sum(scaled, axis=1, keepdims=True) * scale
    second = jnp.sum(scaled * standard, axis=1, keepdims=True) * scale
    out_ref[...] = cot_ref[...] + inv_std * (scaled - first - standard * second)


def shape(*dims, dtype=F32):
    return jax.ShapeDtypeStruct(dims, dtype)


def tiles(array, reverse=False, column=None, tile=TILE):
    width = array.shape[1] if column is None else column

    def index(i, *ids):
        row = array.shape[0] // tile - 1 - i if reverse else i
        return (row, 0 if column is None else ids[0][0])

    return pl.BlockSpec((tile, width), index)


def fixed(array):
    return pl.BlockSpec(array.shape, lambda i, *ids: (0,) * len(array.shape))


ANYWHERE = pl.BlockSpec(memory_space=pl.ANY)


def call(us, kernel, steps, ids, ins, outs, scratch, deps=(), vmem=VMEM_LIMIT):
    in_specs = [fixed(a) if spec is None else spec for a, spec in ins] + [ANYWHERE] * len(deps)
    skip = len(ins) + (ids is not None)

    def bare(*refs):
        kernel(*refs[:skip], *refs[skip + len(deps) :])

    out_specs = [fixed(a) if spec is None else spec for a, spec in outs]
    spec = pltpu.PrefetchScalarGridSpec(
        num_scalar_prefetch=0 if ids is None else 1,
        grid=(steps,),
        in_specs=in_specs,
        out_specs=out_specs,
        scratch_shapes=[pltpu.VMEM(s, d) for s, d in scratch],
    )
    run = pl.pallas_call(
        bare,
        grid_spec=spec,
        out_shape=[a for a, _ in outs],
        compiler_params=pltpu.CompilerParams(vmem_limit_bytes=vmem),
        cost_estimate=pl.CostEstimate(flops=int(us * RATE), bytes_accessed=int(us * COST), transcendentals=0),
    )
    arrays = [a for a, _ in ins] + list(deps)
    return run(*arrays) if ids is None else run(ids, *arrays)


def after(value, *others):
    return lax.optimization_barrier((value,) + others)[0]


def wa_swap(value, distance):
    count = lax.axis_size("wa")
    return lax.ppermute(value, "wa", [(i, i ^ distance) for i in range(count)])


def seq_swap(value, distance):
    count = lax.axis_size("seq")
    return lax.ppermute(value, "seq", [(i, i ^ distance) for i in range(count)])


def seq_shift(value, hop):
    count = lax.axis_size("seq")
    pairs = [(i, i + hop) for i in range(count) if 0 <= i + hop < count]
    return lax.ppermute(value, "seq", pairs)


def block_order(bits):
    count = lax.axis_size("seq")
    if count != 8:
        return jnp.arange(count, dtype=jnp.int32)
    order = [
        sum(bit for k, bit in enumerate(bits) if place >> (2 - k) & 1) for place in range(8)
    ]
    return jnp.array(order, jnp.int32) ^ lax.axis_index("seq")


class ScatterSum:
    def __init__(self, keep, send, bits):
        self.bits = bits
        if lax.axis_size("seq") != 8:
            whole = jnp.concatenate([keep, send], axis=0)
            whole = whole.reshape(-1, whole.shape[2])
            self.total = lax.psum_scatter(whole, "seq", scatter_dimension=0, tiled=True)
            self.keep = None
            return
        self.keep = keep
        self.recv = seq_swap(send, bits[0])

    def step(self, bit, token):
        if self.keep is None:
            return token
        recv = after(self.recv, token)
        half = self.keep.shape[0] // 2
        send = self.keep[half:] + recv[half:]
        self.keep = self.keep[:half] + recv[:half]
        self.recv = seq_swap(send, bit)
        return send

    def finish(self):
        if self.keep is None:
            return self.total
        return (self.keep + self.recv)[0]


def body(
    inputs,
    seq_starts,
    ln_gain,
    ln_bias,
    w_gate,
    b_gate,
    w_reduce,
    b_reduce,
    ssm_rate,
    ssm_step,
    ssm_out,
    w_expand,
    b_expand,
    w_down,
    b_down,
    cotangent,
):
    rows, width = inputs.shape
    part = cotangent.shape[1]
    units = w_gate.shape[1]
    own = w_reduce.shape[1]
    channels = w_expand.shape[0]
    seqs = lax.axis_size("seq")
    steps = rows // TILE
    hops = min(seqs - 1, (SEQ_MAX - 2 + rows) // rows)
    here = lax.axis_index("wa").astype(jnp.int32)
    place = lax.axis_index("seq").astype(jnp.int32)

    def ids_of(bits):
        return jnp.concatenate([jnp.stack([here, place]), block_order(bits)])

    ids = ids_of((1, 2, 4))
    ids_z = ids_of((2, 1, 4))
    gain, shift, b_gate, b_red, rate, step, out_rate, b_exp, b_down_row = (
        v[None] for v in (ln_gain, ln_bias, b_gate, b_reduce, ssm_rate, ssm_step, ssm_out, b_expand, b_down)
    )
    mask = jnp.broadcast_to(1.0 - seq_starts.astype(F32)[:, None], (rows, 128))

    def t(*dims, dtype=F32):
        return shape(rows, *dims, dtype=dtype)

    def tiled(*arrays):
        return [(a, tiles(a)) for a in arrays]

    def whole(*arrays):
        return [(a, None) for a in arrays]

    cot_y = wa_swap(cotangent, 2)
    cot_c = wa_swap(cotangent, 1)

    n_high, n_low, reduced, red_slope, local, lead, end = call(
        7,
        reduce_kernel,
        steps,
        None,
        tiled(inputs) + whole(gain, shift, w_reduce, b_red, rate, step) + tiled(mask),
        tiled(t(width, dtype=BF16), t(width, dtype=BF16), t(own), t(own), t(own), t(own)) + whole(shape(8, own)),
        [((width, own), BF16)] * 2 + [((TILE, own), F32), ((16, own), F32)],
    )
    gots = [seq_shift(end, hop) for hop in range(1, hops + 1)]
    act, slope = call(
        12,
        gate_kernel,
        steps,
        None,
        tiled(n_high, n_low) + whole(w_gate, b_gate),
        tiled(t(units), t(units)),
        [((width, units), BF16)] * 2,
    )
    mixed, states, turn = call(
        2,
        functools.partial(states_kernel, hops),
        steps,
        None,
        tiled(local, lead, reduced, mask) + whole(out_rate, *gots),
        tiled(t(own), t(own), t(own)),
        [((8, own), F32)],
        [act],
    )
    mixed_y = wa_swap(after(mixed, cot_y), 2)
    mixed_c = wa_swap(mixed, 1)
    cot_yc = wa_swap(after(cot_y, mixed), 1)
    cots = [cotangent, cot_c, cot_y, cot_yc]

    c_high, c_low, grad_product, ge_high, ge_low, back_send, c_sum = call(
        17,
        cotangent_kernel,
        steps,
        ids,
        tiled(*cots) + whole(w_down) + tiled(act) + whole(w_expand),
        tiled(
            t(width, dtype=BF16), t(width, dtype=BF16), t(units), t(units, dtype=BF16), t(units, dtype=BF16),
            t(2 * own),
        )
        + whole(shape(8, width)),
        [((width, units), BF16)] * 2 + [((2 * own, units), BF16)] * 2,
        [mixed],
    )
    back_recv = wa_swap(back_send, 1)
    back_keep, ge_sum = call(
        FILL,
        back_kernel,
        steps,
        ids,
        tiled(ge_high, ge_low) + whole(w_expand),
        tiled(t(2 * own)) + whole(shape(8, units)),
        [((2 * own, units), BF16)] * 2,
        [back_send],
    )
    back_far = back_keep[:, :own] + back_recv[:, :own]
    back_y = wa_swap(back_far, 2)

    mixed_yc = wa_swap(after(mixed_y, back_keep), 1)
    m_high, m_low, p_high, p_low, gg_high, gg_low, out_send, out_keep, gg_sum = call(
        14,
        expand_kernel,
        steps,
        ids,
        tiled(mixed, mixed_c, mixed_y, mixed_yc)
        + whole(w_expand, b_exp, w_down)
        + tiled(act, slope, grad_product),
        tiled(
            t(channels, dtype=BF16), t(channels, dtype=BF16), t(units, dtype=BF16), t(units, dtype=BF16),
            t(units, dtype=BF16), t(units, dtype=BF16), t(part), t(part),
        )
        + whole(shape(8, units)),
        [((channels, units), BF16)] * 2 + [((2 * part, units), BF16)] * 2,
        [back_far],
    )
    out_recv = wa_swap(out_send, 1)
    near_send, near_keep = call(
        6.5,
        output_kernel,
        steps,
        ids,
        tiled(p_high, p_low)
        + whole(w_down)
        + [(inputs, tiles(inputs, column=part)), (b_down_row, pl.BlockSpec((1, part), lambda i, ids: (0, ids[0])))],
        tiled(t(part), t(part)),
        [((2 * part, units), BF16)] * 2,
        [out_send],
    )
    out_far = after(out_keep, near_keep) + out_recv
    out_y = wa_swap(out_far, 2)
    near_recv = wa_swap(near_send, 1)

    def backwards(*arrays):
        return [(a, tiles(a, True)) for a in arrays]

    local_back, tail, back_end, out_sum = call(
        1.5,
        adjoint_kernel,
        steps,
        None,
        backwards(back_keep, back_recv, back_y, states, mask) + whole(out_rate, rate, step),
        backwards(t(own), t(own)) + whole(shape(8, own), shape(8, own)),
        [((16, own), F32)],
        [near_keep],
    )
    back_gots = [seq_shift(back_end, -hop) for hop in range(1, hops + 1)]

    def weight(left, right, ids, relative, deps):
        blocks = left[0].shape[1] // seqs
        half = shape(seqs // 2, blocks, right[0].shape[1])
        tile = 2 * TILE
        return call(
            10,
            functools.partial(weight_kernel, relative),
            rows // tile,
            ids,
            [(a, tiles(a, tile=tile)) for a in (*left, *right)],
            whole(half, half),
            [((left[0].shape[1], right[0].shape[1]), F32)],
            deps,
        )

    w_down_keep, w_down_send = weight((c_high, c_low), (p_high, p_low), ids, True, [back_end, out_far])
    down_sum = ScatterSum(w_down_keep, after(w_down_send, *back_gots), (1, 2, 4))
    r_high, r_low, far_send, far_keep, turn_sum, red_sum, far_norm = call(
        8,
        functools.partial(normed_far_kernel, hops),
        steps,
        ids,
        tiled(local_back, tail, turn, red_slope, gg_high, gg_low, inputs)
        + whole(w_gate, w_reduce, rate, step)
        + whole(*back_gots),
        tiled(t(own, dtype=BF16), t(own, dtype=BF16), t(part), t(part))
        + whole(shape(8, own), shape(8, own), shape(16, width)),
        [((2 * part, units), BF16)] * 2 + [((2 * part, own), BF16)] * 2 + [((TILE, width), F32)],
        [w_down_keep],
    )
    far_recv = wa_swap(far_send, 1)
    next_send, next_keep, norm = call(
        7,
        normed_near_kernel,
        steps,
        ids,
        tiled(r_high, r_low, gg_high, gg_low, inputs) + whole(w_gate, w_reduce, far_norm),
        tiled(t(part), t(part)) + whole(shape(8, width)),
        [((2 * part, units), BF16)] * 2
        + [((2 * part, own), BF16)] * 2
        + [((TILE, width), F32), ((16, width), F32)],
        [far_keep],
    )
    far_sum = after(far_keep, next_keep) + far_recv
    far_y = wa_swap(far_sum, 2)
    next_recv = wa_swap(next_send, 1)
    near_sum = after(next_keep, far_sum) + next_recv
    norm_c = wa_swap(norm, 1)
    norm_y = wa_swap(norm, 2)
    norm_yc = wa_swap(norm, 3)

    w_gate_keep, w_gate_send = weight((n_high, n_low), (gg_high, gg_low), ids_z, False, [near_sum])
    gate_total = ScatterSum(w_gate_keep, w_gate_send, (2, 1, 4))
    output = after(near_keep, w_gate_keep) + near_recv + out_y
    w_expand_keep, w_expand_send = weight((m_high, m_low), (ge_high, ge_low), ids, True, [output])
    expand_total = ScatterSum(w_expand_keep, w_expand_send, (1, 2, 4))

    [vector] = call(
        1.5,
        pack_kernel,
        1,
        None,
        whole(norm, norm_c, norm_y, norm_yc, c_sum, gg_sum, ge_sum, red_sum, turn_sum, out_sum),
        whole(shape(8 * seqs, 128)),
        [((8, max(width, units)), F32), ((8, width), F32)],
        [w_expand_keep],
    )
    half = shape(seqs // 2, width // seqs + 8, own)
    w_red_keep, w_red_send = call(
        5,
        reduce_weight_kernel,
        steps,
        ids,
        tiled(n_high, n_low, r_high, r_low) + whole(vector),
        whole(half, half),
        [((width, own), F32)],
        [w_expand_keep],
    )
    reduce_total = ScatterSum(w_red_keep, w_red_send, (1, 2, 4))

    token = down_sum.step(2, w_red_keep)
    grad_own = after(near_sum, token) + far_y
    all_y = wa_swap(grad_own, 2)
    all_c = wa_swap(grad_own, 1)
    all_yc = wa_swap(all_y, 1)
    token = gate_total.step(1, grad_own)
    token = expand_total.step(2, token)
    token = reduce_total.step(2, token)
    token = down_sum.step(4, token)
    token = gate_total.step(4, token)
    token = expand_total.step(4, token)
    token = reduce_total.step(4, token)

    total_w_down = down_sum.finish()
    total_w_gate = gate_total.finish()
    total_w_expand = expand_total.finish()
    total = reduce_total.finish()
    matrix_rows = width // seqs

    def vector_of(k, length):
        return total[matrix_rows + k, : length // seqs]

    count = own // seqs
    rate_here = lax.dynamic_slice_in_dim(ssm_rate, place * count, count, 0)
    step_here = lax.dynamic_slice_in_dim(ssm_step, place * count, count, 0)
    keep_sum = vector_of(6, own)
    grad_log = -keep_sum * jnp.exp(-rate_here * step_here)
    [grad_inputs] = call(
        9,
        final_kernel,
        steps,
        ids,
        tiled(inputs) + whole(gain) + tiled(grad_own, all_c, all_y, all_yc, *cots),
        tiled(t(width)),
        [((TILE, width), F32)] * 2,
    )
    return (
        output,
        grad_inputs,
        vector_of(0, width),
        vector_of(1, width),
        total_w_gate,
        vector_of(3, units),
        total[:matrix_rows],
        vector_of(5, own),
        grad_log * step_here,
        grad_log * rate_here,
        vector_of(7, own),
        total_w_expand,
        vector_of(4, units),
        total_w_down,
        vector_of(2, width),
    )


def solution(mesh):
    in_specs = (
        P("seq", None),
        P("seq"),
        P(),
        P(),
        P(None, "wa"),
        P("wa"),
        P(None, "wa"),
        P("wa"),
        P("wa"),
        P("wa"),
        P("wa"),
        P(None, "wa"),
        P("wa"),
        P(None, "wa"),
        P(),
        P("seq", "wa"),
    )
    out_specs = (
        P("seq", "wa"),
        P("seq", None),
        P("seq"),
        P("seq"),
        P("seq", "wa"),
        P(("wa", "seq")),
        P("seq", "wa"),
        P(("wa", "seq")),
        P(("wa", "seq")),
        P(("wa", "seq")),
        P(("wa", "seq")),
        P("seq", "wa"),
        P(("wa", "seq")),
        P("seq", "wa"),
        P("seq"),
    )
    return jax.shard_map(body, mesh=mesh, in_specs=in_specs, out_specs=out_specs, check_vma=False)
```

```python
import functools

import jax
import jax.numpy as jnp
from jax import lax
from jax.experimental import pallas as pl
from jax.experimental.pallas import tpu as pltpu
from jax.sharding import PartitionSpec as P

EPSILON = 1e-05
INV_ROOT_TAU = 0.3989422804014327
SEQ_MAX = 4096
F32 = jnp.float32
BF16 = jnp.bfloat16
VMEM_LIMIT = 22 * 2**20
TILE = 256
COST = 10**5
RATE = 5 * 10**7
FILL = 400
NN = ((1,), (0,))
NT = ((1,), (1,))
TN = ((0,), (0,))


def split(value):
    high = value.astype(BF16)
    return high, (value - high.astype(F32)).astype(BF16)


def dot(left, right, dims):
    return lax.dot_general(left, right, (dims, ((), ())), preferred_element_type=F32)


def dot3(left, right, dims):
    (left_high, left_low), (right_high, right_low) = left, right
    return dot(left_high, right_high, dims) + (
        dot(left_high, right_low, dims) + dot(left_low, right_high, dims)
    )


def gelu_parts(v):
    bell = jnp.exp(-0.5 * v * v)
    span = 1.0 + 0.23164189 * jnp.abs(v)
    t = pl.reciprocal(span, approx=True)
    t = t * (2.0 - span * t)
    tail = 0.5 * (1.061405429 * t - 1.453152027)
    tail = tail * t + 0.5 * 1.421413741
    tail = tail * t - 0.5 * 0.284496736
    tail = tail * t + 0.5 * 0.254829592
    tail = tail * t * bell
    cdf = jnp.where(v < 0.0, tail, 1.0 - tail)
    return v * cdf, cdf + (INV_ROOT_TAU * v) * bell


def standardise(values):
    scale = 1.0 / values.shape[1]
    centred = values - jnp.sum(values, axis=1, keepdims=True) * scale
    variance = jnp.sum(centred * centred, axis=1, keepdims=True) * scale
    inv_std = lax.rsqrt(variance + EPSILON)
    return centred * inv_std, inv_std


def row_sums(value):
    return jnp.sum(value.reshape(value.shape[0] // 8, 8, value.shape[1]), axis=0)


def sublane(shape=(8, 128)):
    return lax.broadcasted_iota(jnp.int32, shape, 0)


def wide(row):
    return jnp.broadcast_to(row, (8, row.shape[1]))


def entering(gots):
    total = gots[0][0:1, :]
    keep = gots[0][1:2, :]
    for got in gots[1:]:
        total = total + keep * got[0:1, :]
        keep = keep * got[1:2, :]
    return total


def first_step():
    return pl.program_id(0) == 0


def last_step():
    return pl.program_id(0) == pl.num_programs(0) - 1


def apart():
    return pl.when(pl.program_id(0) >= 0)


def add_to(ref, value):
    @pl.when(first_step())
    def _():
        ref[...] = jnp.zeros_like(ref)

    ref[...] += value


def split_rows(ids_ref, order, source_ref, high, low):
    width = high.shape[0] // len(order)
    for place, r in enumerate(order):
        at = pl.multiple_of((ids_ref[0] ^ r) * width, width)
        to = slice(place * width, (place + 1) * width)
        high[to, :], low[to, :] = split(source_ref[pl.ds(at, width), :])


def reduce_kernel(
    x_ref, gain_ref, shift_ref, w_ref, b_ref, rate_ref, step_ref, mask_ref,
    high_ref, low_ref, red_ref, slope_ref, local_ref, lead_ref, end_ref,
    w_high, w_low, drive_ref, carry_ref,
):
    log_keep = -rate_ref[...] * step_ref[...]
    keep = wide(jnp.exp(log_keep))
    fresh = 1.0 - jnp.exp(log_keep)

    @pl.when(first_step())
    def _():
        w_high[...], w_low[...] = split(w_ref[...])
        carry_ref[0:8, :] = jnp.zeros((8, 128), F32)
        carry_ref[8:16, :] = jnp.ones((8, 128), F32)

    standard, _ = standardise(x_ref[...])
    parts = split(standard * gain_ref[...] + shift_ref[...])
    high_ref[...], low_ref[...] = parts
    pre = dot3(parts, (w_high[...], w_low[...]), NN) + b_ref[...]
    reduced, slope_ref[...] = gelu_parts(pre)
    red_ref[...] = reduced
    drive_ref[...] = fresh * reduced
    at = sublane()
    powers = [keep, keep * keep]
    powers.append(powers[1] * powers[1])
    ramp = jnp.exp((at + 1).astype(F32) * log_keep)

    def step(j, carry):
        state, decay = carry
        here = pl.ds(pl.multiple_of(j * 8, 8), 8)
        value = drive_ref[here, :]
        mask = mask_ref[here, :]
        for power, hop in zip(powers, (1, 2, 4)):
            inside = at >= hop
            value = value + jnp.where(inside, power * mask, 0.0) * pltpu.roll(value, hop, 0)
            mask = jnp.where(inside, mask * pltpu.roll(mask, hop, 0), mask)
        factor = ramp * mask
        value = value + factor * state
        factor = factor * decay
        local_ref[here, :] = value
        lead_ref[here, :] = factor
        return (wide(value[7:8, :]), wide(factor[7:8, :]))

    start = (carry_ref[0:8, :], carry_ref[8:16, :])
    state, decay = lax.fori_loop(0, x_ref.shape[0] // 8, step, start, unroll=8)
    carry_ref[0:8, :] = state
    carry_ref[8:16, :] = decay
    end_ref[...] = jnp.where(at == 0, state, decay)


def gate_kernel(high_ref, low_ref, w_ref, b_ref, act_ref, slope_ref, w_high, w_low):
    @pl.when(first_step())
    def _():
        w_high[...], w_low[...] = split(w_ref[...])

    pre = dot3((high_ref[...], low_ref[...]), (w_high[...], w_low[...]), NN) + b_ref[...]
    act_ref[...], slope_ref[...] = gelu_parts(pre)


def states_kernel(hops, local_ref, lead_ref, red_ref, mask_ref, out_ref, *rest):
    gots, (mixed_ref, states_ref, turn_ref, last_ref) = rest[:hops], rest[hops:]
    enter = entering(gots)

    @pl.when(first_step())
    def _():
        last_ref[...] = wide(enter)

    states = local_ref[...] + lead_ref[...] * enter
    states_ref[...] = states
    mixed_ref[...] = states * out_ref[...]
    first = sublane(states.shape) == 0
    before = jnp.where(first, last_ref[0:1, :], pltpu.roll(states, 1, 0))
    turn_ref[...] = mask_ref[...] * before - red_ref[...]
    last_ref[...] = wide(states[states.shape[0] - 1 :, :])


def cotangent_kernel(
    ids_ref, c0, c1, c2, c3, wd_ref, act_ref, we_ref,
    high_ref, low_ref, gp_ref, ge_high, ge_low, send_ref, c_sum,
    wd_high, wd_low, we_high, we_low,
):
    width = c0.shape[1]

    @pl.when(first_step())
    def _():
        split_rows(ids_ref, range(4), wd_ref, wd_high, wd_low)
        split_rows(ids_ref, (3, 1), we_ref, we_high, we_low)

    for r, c in enumerate((c0, c1, c2, c3)):
        at = slice(r * width, (r + 1) * width)
        high_ref[:, at], low_ref[:, at] = split(c[...])
        add_to(c_sum.at[:, at], row_sums(c[...]))
    grad_product = dot3((high_ref[...], low_ref[...]), (wd_high[...], wd_low[...]), NN)
    gp_ref[...] = grad_product
    ge_high[...], ge_low[...] = split(grad_product * act_ref[...])

    @apart()
    def _():
        send_ref[...] = dot3((ge_high[...], ge_low[...]), (we_high[...], we_low[...]), NT)


def back_kernel(ids_ref, ge_high, ge_low, we_ref, keep_ref, ge_sum, we_high, we_low):
    @pl.when(first_step())
    def _():
        split_rows(ids_ref, (2, 0), we_ref, we_high, we_low)

    keep_ref[...] = dot3((ge_high[...], ge_low[...]), (we_high[...], we_low[...]), NT)
    add_to(ge_sum, row_sums(ge_high[...].astype(F32) + ge_low[...].astype(F32)))


def expand_kernel(
    ids_ref, m0, m1, m2, m3, we_ref, be_ref, act_ref, slope_ref, gp_ref,
    mix_high, mix_low, prod_high, prod_low, gate_high, gate_low, gate_sum, we_high, we_low,
):
    own = m0.shape[1]

    @pl.when(first_step())
    def _():
        split_rows(ids_ref, range(4), we_ref, we_high, we_low)

    for r, m in enumerate((m0, m1, m2, m3)):
        at = slice(r * own, (r + 1) * own)
        mix_high[:, at], mix_low[:, at] = split(m[...])
    expand = dot3((mix_high[...], mix_low[...]), (we_high[...], we_low[...]), NN) + be_ref[...]
    prod_high[...], prod_low[...] = split(act_ref[...] * expand)
    grad_gate = gp_ref[...] * expand * slope_ref[...]
    gate_high[...], gate_low[...] = split(grad_gate)
    add_to(gate_sum, row_sums(grad_gate))


def output_kernel(
    ids_ref, high_ref, low_ref, wd_ref, x_ref, b_ref, far_send, far_keep, near_send, near_keep, wd_high, wd_low
):
    width = near_keep.shape[1]

    @pl.when(first_step())
    def _():
        split_rows(ids_ref, (3, 2, 1, 0), wd_ref, wd_high, wd_low)

    out = dot3((high_ref[...], low_ref[...]), (wd_high[...], wd_low[...]), NT)
    far_send[...] = out[:, :width]
    far_keep[...] = out[:, width : 2 * width]
    near_send[...] = out[:, 2 * width : 3 * width]
    near_keep[...] = out[:, 3 * width :] + x_ref[...] + b_ref[...]


def adjoint_kernel(
    keep_ref, recv_ref, far_ref, states_ref, mask_ref, out_ref, rate_ref, step_ref,
    local_ref, tail_ref, end_ref, sum_ref, carry_ref,
):
    own = far_ref.shape[1]
    log_keep = -rate_ref[...] * step_ref[...]
    keep = wide(jnp.exp(log_keep))

    @pl.when(first_step())
    def _():
        carry_ref[0:8, :] = jnp.zeros((8, 128), F32)
        carry_ref[8:16, :] = jnp.ones((8, 128), F32)

    at = sublane()
    powers = [keep, keep * keep]
    powers.append(powers[1] * powers[1])
    ramp = jnp.exp((8 - at).astype(F32) * log_keep)
    out_rate = wide(out_ref[...])
    count = far_ref.shape[0] // 8

    def step(n, carry):
        state, decay, total = carry
        here = pl.ds(pl.multiple_of((count - 1 - n) * 8, 8), 8)
        grad = keep_ref[here, own:] + recv_ref[here, own:] + far_ref[here, :]
        total = total + grad * states_ref[here, :]
        drive = grad * out_rate
        mask = mask_ref[here, :]
        value = keep * mask * drive
        for power, hop in zip(powers, (1, 2, 4)):
            inside = at < 8 - hop
            value = value + jnp.where(inside, power * mask, 0.0) * pltpu.roll(value, 8 - hop, 0)
            mask = jnp.where(inside, mask * pltpu.roll(mask, 8 - hop, 0), mask)
        factor = ramp * mask
        value = value + factor * state
        factor = factor * decay
        local_ref[here, :] = drive + jnp.where(at == 7, state, pltpu.roll(value, 7, 0))
        tail_ref[here, :] = jnp.where(at == 7, decay, pltpu.roll(factor, 7, 0))
        return (wide(value[0:1, :]), wide(factor[0:1, :]), total)

    start = (carry_ref[0:8, :], carry_ref[8:16, :], jnp.zeros((8, 128), F32))
    state, decay, total = lax.fori_loop(0, count, step, start, unroll=8)
    carry_ref[0:8, :] = state
    carry_ref[8:16, :] = decay
    end_ref[...] = jnp.where(at == 0, state, decay)
    add_to(sum_ref, total)


def add_norm_sums(ids_ref, x_ref, parts, standard_ref, sums_ref):
    width = parts[0][1].shape[1]
    standard_ref[...], _ = standardise(x_ref[...])
    for r, part in parts:
        at = pl.ds(pl.multiple_of((ids_ref[0] ^ r) * width, width), width)
        sums_ref[0:8, at] += row_sums(part * standard_ref[:, at])
        sums_ref[8:16, at] += row_sums(part)


def normed_far_kernel(
    hops, ids_ref, local_ref, tail_ref, turn_ref, slope_ref, gate_high, gate_low, x_ref,
    wg_ref, wr_ref, rate_ref, step_ref, *rest,
):
    gots = rest[:hops]
    (red_high, red_low, send_ref, keep_ref, turn_sum, red_sum, norm_sum,
     wg_high, wg_low, wr_high, wr_low, standard_ref) = rest[hops:]
    width = send_ref.shape[1]

    @pl.when(first_step())
    def _():
        split_rows(ids_ref, (3, 2), wg_ref, wg_high, wg_low)
        split_rows(ids_ref, (3, 2), wr_ref, wr_high, wr_low)
        norm_sum[...] = jnp.zeros_like(norm_sum)

    adjoint = local_ref[...] + tail_ref[...] * entering(gots)
    fresh = 1.0 - jnp.exp(-rate_ref[...] * step_ref[...])
    grad = fresh * adjoint * slope_ref[...]
    parts = split(grad)
    red_high[...], red_low[...] = parts
    add_to(turn_sum, row_sums(adjoint * turn_ref[...]))
    add_to(red_sum, row_sums(grad))
    back = dot3((gate_high[...], gate_low[...]), (wg_high[...], wg_low[...]), NT)
    back = back + dot3(parts, (wr_high[...], wr_low[...]), NT)
    send_ref[...] = back[:, :width]
    keep_ref[...] = back[:, width:]
    add_norm_sums(ids_ref, x_ref, [(3, back[:, :width]), (2, back[:, width:])], standard_ref, norm_sum)


def normed_near_kernel(
    ids_ref, red_high, red_low, gate_high, gate_low, x_ref, wg_ref, wr_ref, far_sum,
    send_ref, keep_ref, norm_ref, wg_high, wg_low, wr_high, wr_low, standard_ref, norm_sum,
):
    width = send_ref.shape[1]

    @pl.when(first_step())
    def _():
        split_rows(ids_ref, (1, 0), wg_ref, wg_high, wg_low)
        split_rows(ids_ref, (1, 0), wr_ref, wr_high, wr_low)
        norm_sum[...] = far_sum[...]

    back = dot3((gate_high[...], gate_low[...]), (wg_high[...], wg_low[...]), NT)
    back = back + dot3((red_high[...], red_low[...]), (wr_high[...], wr_low[...]), NT)
    send_ref[...] = back[:, :width]
    keep_ref[...] = back[:, width:]
    add_norm_sums(ids_ref, x_ref, [(1, back[:, :width]), (0, back[:, width:])], standard_ref, norm_sum)

    @pl.when(last_step())
    def _():
        gain = jnp.sum(norm_sum[0:8, :], axis=0, keepdims=True)
        shift = jnp.sum(norm_sum[8:16, :], axis=0, keepdims=True)
        norm_ref[...] = jnp.where(sublane(norm_ref.shape) == 0, gain, shift)


def weight_kernel(relative, ids_ref, left_high, left_low, right_high, right_low, keep_ref, send_ref, acc_ref):
    @pl.when(first_step())
    def _():
        acc_ref[...] = jnp.zeros_like(acc_ref)

    for at in range(0, acc_ref.shape[1], 256):
        to = slice(at, at + 256)
        acc_ref[:, to] += dot3((left_high[...], left_low[...]), (right_high[:, to], right_low[:, to]), TN)
    half, rows, _ = keep_ref.shape
    block = acc_ref.shape[0] // 4

    @pl.when(last_step())
    def _():
        for place in range(2 * half):
            at = ids_ref[2 + place] * rows
            if relative:
                at = ((at // block) ^ ids_ref[0]) * block + at % block
            value = acc_ref[pl.ds(pl.multiple_of(at, 8), rows), :]
            if place < half:
                keep_ref[place] = value
            else:
                send_ref[place - half] = value


def reduce_weight_kernel(
    ids_ref, left_high, left_low, right_high, right_low, vector_ref, keep_ref, send_ref, acc_ref
):
    add_to(acc_ref, dot3((left_high[...], left_low[...]), (right_high[...], right_low[...]), TN))
    half, rows, _ = keep_ref.shape
    rows = rows - 8

    @pl.when(last_step())
    def _():
        for place in range(2 * half):
            block = ids_ref[2 + place]
            to, slot = (keep_ref, place) if place < half else (send_ref, place - half)
            to[slot, :rows] = acc_ref[pl.ds(pl.multiple_of(block * rows, 8), rows), :]
            to[slot, rows:] = vector_ref[pl.ds(pl.multiple_of(block * 8, 8), 8), :]


def pack_kernel(norm_ref, down_ref, gate_ref, expand_ref, red_ref, turn_ref, out_ref,
                vector_ref, whole_ref, here_ref):
    count = vector_ref.shape[0] // 8
    vector_ref[...] = jnp.zeros_like(vector_ref)
    width = down_ref.shape[1] // 4
    here = lax.axis_index("wa")
    for r in range(4):
        at = pl.multiple_of((here ^ r) * width, width)
        here_ref[2:3, pl.ds(at, width)] = jnp.sum(down_ref[:, r * width : (r + 1) * width], axis=0, keepdims=True)
    here_ref[0:2, :] = norm_ref[0:2, :]
    rows = [here_ref[0:1, :], here_ref[1:2, :], here_ref[2:3, :]]
    rows += [jnp.sum(ref[...], axis=0, keepdims=True) for ref in (gate_ref, expand_ref, red_ref, turn_ref, out_ref)]
    for k, row in enumerate(rows):
        whole_ref[k : k + 1, : row.shape[1]] = row
    for k, row in enumerate(rows):
        size = row.shape[1] // count
        for d in range(count):
            vector_ref[d * 8 + k : d * 8 + k + 1, :size] = whole_ref[k : k + 1, d * size : (d + 1) * size]


def final_kernel(ids_ref, x_ref, gain_ref, g0, g1, g2, g3, c0, c1, c2, c3, out_ref, grad_ref, cot_ref):
    width = g0.shape[1]
    for r, (g, c) in enumerate(((g0, c0), (g1, c1), (g2, c2), (g3, c3))):
        at = pl.ds(pl.multiple_of((ids_ref[0] ^ r) * width, width), width)
        grad_ref[:, at] = g[...]
        cot_ref[:, at] = c[...]
    scale = 1.0 / x_ref.shape[1]
    standard, inv_std = standardise(x_ref[...])
    scaled = grad_ref[...] * gain_ref[...]
    first = jnp.sum(scaled, axis=1, keepdims=True) * scale
    second = jnp.sum(scaled * standard, axis=1, keepdims=True) * scale
    out_ref[...] = cot_ref[...] + inv_std * (scaled - first - standard * second)


def shape(*dims, dtype=F32):
    return jax.ShapeDtypeStruct(dims, dtype)


def tiles(array, reverse=False, column=None, tile=TILE):
    width = array.shape[1] if column is None else column

    def index(i, *ids):
        row = array.shape[0] // tile - 1 - i if reverse else i
        return (row, 0 if column is None else ids[0][0])

    return pl.BlockSpec((tile, width), index)


def fixed(array):
    return pl.BlockSpec(array.shape, lambda i, *ids: (0,) * len(array.shape))


ANYWHERE = pl.BlockSpec(memory_space=pl.ANY)


def call(us, kernel, steps, ids, ins, outs, scratch, deps=(), vmem=VMEM_LIMIT):
    in_specs = [fixed(a) if spec is None else spec for a, spec in ins] + [ANYWHERE] * len(deps)
    skip = len(ins) + (ids is not None)

    def bare(*refs):
        kernel(*refs[:skip], *refs[skip + len(deps) :])

    out_specs = [fixed(a) if spec is None else spec for a, spec in outs]
    spec = pltpu.PrefetchScalarGridSpec(
        num_scalar_prefetch=0 if ids is None else 1,
        grid=(steps,),
        in_specs=in_specs,
        out_specs=out_specs,
        scratch_shapes=[pltpu.VMEM(s, d) for s, d in scratch],
    )
    run = pl.pallas_call(
        bare,
        grid_spec=spec,
        out_shape=[a for a, _ in outs],
        compiler_params=pltpu.CompilerParams(vmem_limit_bytes=vmem),
        cost_estimate=pl.CostEstimate(flops=int(us * RATE), bytes_accessed=int(us * COST), transcendentals=0),
    )
    arrays = [a for a, _ in ins] + list(deps)
    return run(*arrays) if ids is None else run(ids, *arrays)


def after(value, *others):
    return lax.optimization_barrier((value,) + others)[0]


def wa_swap(value, distance):
    count = lax.axis_size("wa")
    return lax.ppermute(value, "wa", [(i, i ^ distance) for i in range(count)])


def seq_swap(value, distance):
    count = lax.axis_size("seq")
    return lax.ppermute(value, "seq", [(i, i ^ distance) for i in range(count)])


def seq_shift(value, hop):
    count = lax.axis_size("seq")
    pairs = [(i, i + hop) for i in range(count) if 0 <= i + hop < count]
    return lax.ppermute(value, "seq", pairs)


def block_order(bits):
    count = lax.axis_size("seq")
    if count != 8:
        return jnp.arange(count, dtype=jnp.int32)
    order = [
        sum(bit for k, bit in enumerate(bits) if place >> (2 - k) & 1) for place in range(8)
    ]
    return jnp.array(order, jnp.int32) ^ lax.axis_index("seq")


class ScatterSum:
    def __init__(self, keep, send, bits):
        self.bits = bits
        if lax.axis_size("seq") != 8:
            whole = jnp.concatenate([keep, send], axis=0)
            whole = whole.reshape(-1, whole.shape[2])
            self.total = lax.psum_scatter(whole, "seq", scatter_dimension=0, tiled=True)
            self.keep = None
            return
        self.keep = keep
        self.recv = seq_swap(send, bits[0])

    def step(self, bit, token):
        if self.keep is None:
            return token
        recv = after(self.recv, token)
        half = self.keep.shape[0] // 2
        send = self.keep[half:] + recv[half:]
        self.keep = self.keep[:half] + recv[:half]
        self.recv = seq_swap(send, bit)
        return send

    def finish(self):
        if self.keep is None:
            return self.total
        return (self.keep + self.recv)[0]


def body(
    inputs,
    seq_starts,
    ln_gain,
    ln_bias,
    w_gate,
    b_gate,
    w_reduce,
    b_reduce,
    ssm_rate,
    ssm_step,
    ssm_out,
    w_expand,
    b_expand,
    w_down,
    b_down,
    cotangent,
):
    rows, width = inputs.shape
    part = cotangent.shape[1]
    units = w_gate.shape[1]
    own = w_reduce.shape[1]
    channels = w_expand.shape[0]
    seqs = lax.axis_size("seq")
    steps = rows // TILE
    hops = min(seqs - 1, (SEQ_MAX - 2 + rows) // rows)
    here = lax.axis_index("wa").astype(jnp.int32)
    place = lax.axis_index("seq").astype(jnp.int32)

    def ids_of(bits):
        return jnp.concatenate([jnp.stack([here, place]), block_order(bits)])

    ids = ids_of((1, 2, 4))
    ids_z = ids_of((2, 1, 4))
    gain, shift, b_gate, b_red, rate, step, out_rate, b_exp, b_down_row = (
        v[None] for v in (ln_gain, ln_bias, b_gate, b_reduce, ssm_rate, ssm_step, ssm_out, b_expand, b_down)
    )
    mask = jnp.broadcast_to(1.0 - seq_starts.astype(F32)[:, None], (rows, 128))

    def t(*dims, dtype=F32):
        return shape(rows, *dims, dtype=dtype)

    def tiled(*arrays):
        return [(a, tiles(a)) for a in arrays]

    def whole(*arrays):
        return [(a, None) for a in arrays]

    cot_y = wa_swap(cotangent, 2)
    cot_c = wa_swap(cotangent, 1)

    n_high, n_low, reduced, red_slope, local, lead, end = call(
        7,
        reduce_kernel,
        steps,
        None,
        tiled(inputs) + whole(gain, shift, w_reduce, b_red, rate, step) + tiled(mask),
        tiled(t(width, dtype=BF16), t(width, dtype=BF16), t(own), t(own), t(own), t(own)) + whole(shape(8, own)),
        [((width, own), BF16)] * 2 + [((TILE, own), F32), ((16, own), F32)],
    )
    gots = [seq_shift(end, hop) for hop in range(1, hops + 1)]
    mixed, states, turn = call(
        2,
        functools.partial(states_kernel, hops),
        steps,
        None,
        tiled(local, lead, reduced, mask) + whole(out_rate, *gots),
        tiled(t(own), t(own), t(own)),
        [((8, own), F32)],
    )
    act, slope = call(
        12,
        gate_kernel,
        steps,
        None,
        tiled(n_high, n_low) + whole(w_gate, b_gate),
        tiled(t(units), t(units)),
        [((width, units), BF16)] * 2,
        [mixed],
    )
    mixed_y = wa_swap(mixed, 2)
    mixed_c = wa_swap(mixed, 1)
    cot_yc = wa_swap(after(cot_y, act), 1)
    cots = [cotangent, cot_c, cot_y, cot_yc]

    c_high, c_low, grad_product, ge_high, ge_low, back_send, c_sum = call(
        17,
        cotangent_kernel,
        steps,
        ids,
        tiled(*cots) + whole(w_down) + tiled(act) + whole(w_expand),
        tiled(
            t(width, dtype=BF16), t(width, dtype=BF16), t(units), t(units, dtype=BF16), t(units, dtype=BF16),
            t(2 * own),
        )
        + whole(shape(8, width)),
        [((width, units), BF16)] * 2 + [((2 * own, units), BF16)] * 2,
        [act],
    )
    back_recv = wa_swap(back_send, 1)
    back_keep, ge_sum = call(
        FILL,
        back_kernel,
        steps,
        ids,
        tiled(ge_high, ge_low) + whole(w_expand),
        tiled(t(2 * own)) + whole(shape(8, units)),
        [((2 * own, units), BF16)] * 2,
        [back_send],
    )
    back_far = back_keep[:, :own] + back_recv[:, :own]
    back_y = wa_swap(back_far, 2)

    mixed_yc = wa_swap(after(mixed_y, back_keep), 1)
    m_high, m_low, p_high, p_low, gg_high, gg_low, gg_sum = call(
        9,
        expand_kernel,
        steps,
        ids,
        tiled(mixed, mixed_c, mixed_y, mixed_yc) + whole(w_expand, b_exp) + tiled(act, slope, grad_product),
        tiled(
            t(channels, dtype=BF16), t(channels, dtype=BF16), t(units, dtype=BF16), t(units, dtype=BF16),
            t(units, dtype=BF16), t(units, dtype=BF16),
        )
        + whole(shape(8, units)),
        [((channels, units), BF16)] * 2,
        [back_far],
    )

    def weight(left, right, ids, relative, deps):
        blocks = left[0].shape[1] // seqs
        half = shape(seqs // 2, blocks, right[0].shape[1])
        tile = 2 * TILE
        return call(
            10,
            functools.partial(weight_kernel, relative),
            rows // tile,
            ids,
            [(a, tiles(a, tile=tile)) for a in (*left, *right)],
            whole(half, half),
            [((left[0].shape[1], right[0].shape[1]), F32)],
            deps,
        )

    w_down_keep, w_down_send = weight((c_high, c_low), (p_high, p_low), ids, True, [gg_sum])

    def backwards(*arrays):
        return [(a, tiles(a, True)) for a in arrays]

    local_back, tail, back_end, out_sum = call(
        1.5,
        adjoint_kernel,
        steps,
        None,
        backwards(back_keep, back_recv, back_y, states, mask) + whole(out_rate, rate, step),
        backwards(t(own), t(own)) + whole(shape(8, own), shape(8, own)),
        [((16, own), F32)],
        [w_down_keep],
    )
    back_gots = [seq_shift(back_end, -hop) for hop in range(1, hops + 1)]

    out_send, out_keep, near_send, near_keep = call(
        9,
        output_kernel,
        steps,
        ids,
        tiled(p_high, p_low)
        + whole(w_down)
        + [(inputs, tiles(inputs, column=part)), (b_down_row, pl.BlockSpec((1, part), lambda i, ids: (0, ids[0])))],
        tiled(t(part), t(part), t(part), t(part)),
        [((width, units), BF16)] * 2,
        [back_end],
    )
    down_sum = ScatterSum(w_down_keep, after(w_down_send, *back_gots), (1, 2, 4))
    r_high, r_low, far_send, far_keep, turn_sum, red_sum, far_norm = call(
        8,
        functools.partial(normed_far_kernel, hops),
        steps,
        ids,
        tiled(local_back, tail, turn, red_slope, gg_high, gg_low, inputs)
        + whole(w_gate, w_reduce, rate, step)
        + whole(*back_gots),
        tiled(t(own, dtype=BF16), t(own, dtype=BF16), t(part), t(part))
        + whole(shape(8, own), shape(8, own), shape(16, width)),
        [((2 * part, units), BF16)] * 2 + [((2 * part, own), BF16)] * 2 + [((TILE, width), F32)],
        [near_keep],
    )
    far_recv = wa_swap(far_send, 1)
    next_send, next_keep, norm = call(
        7,
        normed_near_kernel,
        steps,
        ids,
        tiled(r_high, r_low, gg_high, gg_low, inputs) + whole(w_gate, w_reduce, far_norm),
        tiled(t(part), t(part)) + whole(shape(8, width)),
        [((2 * part, units), BF16)] * 2
        + [((2 * part, own), BF16)] * 2
        + [((TILE, width), F32), ((16, width), F32)],
        [far_keep],
    )
    far_sum = after(far_keep, next_keep) + far_recv
    far_y = wa_swap(far_sum, 2)
    next_recv = wa_swap(next_send, 1)
    near_sum = after(next_keep, far_sum) + next_recv

    w_gate_keep, w_gate_send = weight((n_high, n_low), (gg_high, gg_low), ids_z, False, [near_sum])
    gate_total = ScatterSum(w_gate_keep, w_gate_send, (2, 1, 4))
    w_expand_keep, w_expand_send = weight((m_high, m_low), (ge_high, ge_low), ids, True, [w_gate_keep])
    expand_total = ScatterSum(w_expand_keep, w_expand_send, (1, 2, 4))
    token = down_sum.step(2, w_expand_keep)
    grad_own = after(near_sum, token) + far_y
    all_y = wa_swap(grad_own, 2)

    [vector] = call(
        1.5,
        pack_kernel,
        1,
        None,
        whole(norm, c_sum, gg_sum, ge_sum, red_sum, turn_sum, out_sum),
        whole(shape(8 * seqs, 128)),
        [((8, max(width, units)), F32), ((8, width), F32)],
        [grad_own],
    )
    half = shape(seqs // 2, width // seqs + 8, own)
    w_red_keep, w_red_send = call(
        5,
        reduce_weight_kernel,
        steps,
        ids,
        tiled(n_high, n_low, r_high, r_low) + whole(vector),
        whole(half, half),
        [((width, own), F32)],
        [grad_own],
    )
    reduce_total = ScatterSum(w_red_keep, w_red_send, (1, 2, 4))

    out_recv = wa_swap(after(out_send, w_red_keep), 1)
    near_recv = wa_swap(after(near_send, w_red_keep), 1)
    token = gate_total.step(1, w_red_keep)
    token = expand_total.step(2, token)
    out_far = after(out_keep, token) + out_recv
    out_y = wa_swap(after(out_far, all_y), 2)
    near_keep = near_keep + near_recv
    token = down_sum.step(4, out_far)
    token = reduce_total.step(2, token)
    all_c = wa_swap(after(grad_own, token), 1)
    all_yc = wa_swap(after(all_y, token), 1)
    [grad_inputs] = call(
        9,
        final_kernel,
        steps,
        ids,
        tiled(inputs) + whole(gain) + tiled(grad_own, all_c, all_y, all_yc, *cots),
        tiled(t(width)),
        [((TILE, width), F32)] * 2,
        [token],
    )
    output = after(near_keep, grad_inputs) + out_y
    token = gate_total.step(4, grad_inputs)
    token = expand_total.step(4, token)
    token = reduce_total.step(4, token)

    total_w_down = down_sum.finish()
    total_w_gate = gate_total.finish()
    total_w_expand = expand_total.finish()
    total = reduce_total.finish()
    matrix_rows = width // seqs
    norm_sums = total[matrix_rows : matrix_rows + 8]
    norm_sums = norm_sums + wa_swap(norm_sums, 1)
    norm_sums = norm_sums + wa_swap(norm_sums, 2)

    def vector_of(k, length):
        return total[matrix_rows + k, : length // seqs]

    count = own // seqs
    rate_here = lax.dynamic_slice_in_dim(ssm_rate, place * count, count, 0)
    step_here = lax.dynamic_slice_in_dim(ssm_step, place * count, count, 0)
    keep_sum = vector_of(6, own)
    grad_log = -keep_sum * jnp.exp(-rate_here * step_here)
    return (
        output,
        grad_inputs,
        norm_sums[0, : width // seqs],
        norm_sums[1, : width // seqs],
        total_w_gate,
        vector_of(3, units),
        total[:matrix_rows],
        vector_of(5, own),
        grad_log * step_here,
        grad_log * rate_here,
        vector_of(7, own),
        total_w_expand,
        vector_of(4, units),
        total_w_down,
        vector_of(2, width),
    )


def solution(mesh):
    in_specs = (
        P("seq", None),
        P("seq"),
        P(),
        P(),
        P(None, "wa"),
        P("wa"),
        P(None, "wa"),
        P("wa"),
        P("wa"),
        P("wa"),
        P("wa"),
        P(None, "wa"),
        P("wa"),
        P(None, "wa"),
        P(),
        P("seq", "wa"),
    )
    out_specs = (
        P("seq", "wa"),
        P("seq", None),
        P("seq"),
        P("seq"),
        P("seq", "wa"),
        P(("wa", "seq")),
        P("seq", "wa"),
        P(("wa", "seq")),
        P(("wa", "seq")),
        P(("wa", "seq")),
        P(("wa", "seq")),
        P("seq", "wa"),
        P(("wa", "seq")),
        P("seq", "wa"),
        P("seq"),
    )
    return jax.shard_map(body, mesh=mesh, in_specs=in_specs, out_specs=out_specs, check_vma=False)
```

```python
import functools

import jax
import jax.numpy as jnp
from jax import lax
from jax.experimental import pallas as pl
from jax.experimental.pallas import tpu as pltpu
from jax.sharding import PartitionSpec as P

EPSILON = 1e-05
INV_ROOT_TAU = 0.3989422804014327
SEQ_MAX = 4096
F32 = jnp.float32
BF16 = jnp.bfloat16
VMEM_LIMIT = 20 * 2**20
TILE = 256
COST = 10**5
RATE = 5 * 10**7
FILL = 400
NN = ((1,), (0,))
NT = ((1,), (1,))
TN = ((0,), (0,))


def split(value):
    high = value.astype(BF16)
    return high, (value - high.astype(F32)).astype(BF16)


def dot(left, right, dims):
    return lax.dot_general(left, right, (dims, ((), ())), preferred_element_type=F32)


def dot3(left, right, dims):
    (left_high, left_low), (right_high, right_low) = left, right
    return dot(left_high, right_high, dims) + (
        dot(left_high, right_low, dims) + dot(left_low, right_high, dims)
    )


def gelu_parts(v):
    bell = jnp.exp(-0.5 * v * v)
    span = 1.0 + 0.23164189 * jnp.abs(v)
    t = pl.reciprocal(span, approx=True)
    t = t * (2.0 - span * t)
    tail = 0.5 * (1.061405429 * t - 1.453152027)
    tail = tail * t + 0.5 * 1.421413741
    tail = tail * t - 0.5 * 0.284496736
    tail = tail * t + 0.5 * 0.254829592
    tail = tail * t * bell
    cdf = jnp.where(v < 0.0, tail, 1.0 - tail)
    return v * cdf, cdf + (INV_ROOT_TAU * v) * bell


def standardise(values):
    scale = 1.0 / values.shape[1]
    centred = values - jnp.sum(values, axis=1, keepdims=True) * scale
    variance = jnp.sum(centred * centred, axis=1, keepdims=True) * scale
    inv_std = lax.rsqrt(variance + EPSILON)
    return centred * inv_std, inv_std


def row_sums(value):
    return jnp.sum(value.reshape(value.shape[0] // 8, 8, value.shape[1]), axis=0)


def sublane(shape=(8, 128)):
    return lax.broadcasted_iota(jnp.int32, shape, 0)


def wide(row):
    return jnp.broadcast_to(row, (8, row.shape[1]))


def entering(gots):
    total = gots[0][0:1, :]
    keep = gots[0][1:2, :]
    for got in gots[1:]:
        total = total + keep * got[0:1, :]
        keep = keep * got[1:2, :]
    return total


def first_step():
    return pl.program_id(0) == 0


def last_step():
    return pl.program_id(0) == pl.num_programs(0) - 1


def apart():
    return pl.when(pl.program_id(0) >= 0)


def add_to(ref, value):
    @pl.when(first_step())
    def _():
        ref[...] = jnp.zeros_like(ref)

    ref[...] += value


def split_rows(ids_ref, order, source_ref, high, low):
    width = high.shape[0] // len(order)
    for place, r in enumerate(order):
        at = pl.multiple_of((ids_ref[0] ^ r) * width, width)
        to = slice(place * width, (place + 1) * width)
        high[to, :], low[to, :] = split(source_ref[pl.ds(at, width), :])


def reduce_kernel(
    x_ref, gain_ref, shift_ref, w_ref, b_ref, rate_ref, step_ref, mask_ref,
    high_ref, low_ref, red_ref, slope_ref, local_ref, lead_ref, end_ref,
    w_high, w_low, drive_ref, carry_ref,
):
    log_keep = -rate_ref[...] * step_ref[...]
    keep = wide(jnp.exp(log_keep))
    fresh = 1.0 - jnp.exp(log_keep)

    @pl.when(first_step())
    def _():
        w_high[...], w_low[...] = split(w_ref[...])
        carry_ref[0:8, :] = jnp.zeros((8, 128), F32)
        carry_ref[8:16, :] = jnp.ones((8, 128), F32)

    standard, _ = standardise(x_ref[...])
    parts = split(standard * gain_ref[...] + shift_ref[...])
    high_ref[...], low_ref[...] = parts
    pre = dot3(parts, (w_high[...], w_low[...]), NN) + b_ref[...]
    reduced, slope_ref[...] = gelu_parts(pre)
    red_ref[...] = reduced
    drive_ref[...] = fresh * reduced
    at = sublane()
    powers = [keep, keep * keep]
    powers.append(powers[1] * powers[1])
    ramp = jnp.exp((at + 1).astype(F32) * log_keep)

    def step(j, carry):
        state, decay = carry
        here = pl.ds(pl.multiple_of(j * 8, 8), 8)
        value = drive_ref[here, :]
        mask = mask_ref[here, :]
        for power, hop in zip(powers, (1, 2, 4)):
            inside = at >= hop
            value = value + jnp.where(inside, power * mask, 0.0) * pltpu.roll(value, hop, 0)
            mask = jnp.where(inside, mask * pltpu.roll(mask, hop, 0), mask)
        factor = ramp * mask
        value = value + factor * state
        factor = factor * decay
        local_ref[here, :] = value
        lead_ref[here, :] = factor
        return (wide(value[7:8, :]), wide(factor[7:8, :]))

    start = (carry_ref[0:8, :], carry_ref[8:16, :])
    state, decay = lax.fori_loop(0, x_ref.shape[0] // 8, step, start, unroll=8)
    carry_ref[0:8, :] = state
    carry_ref[8:16, :] = decay
    end_ref[...] = jnp.where(at == 0, state, decay)


def gate_kernel(high_ref, low_ref, w_ref, b_ref, act_ref, slope_ref, w_high, w_low):
    @pl.when(first_step())
    def _():
        w_high[...], w_low[...] = split(w_ref[...])

    pre = dot3((high_ref[...], low_ref[...]), (w_high[...], w_low[...]), NN) + b_ref[...]
    act_ref[...], slope_ref[...] = gelu_parts(pre)


def states_kernel(hops, local_ref, lead_ref, red_ref, mask_ref, out_ref, *rest):
    gots, (mixed_ref, states_ref, turn_ref, last_ref) = rest[:hops], rest[hops:]
    enter = entering(gots)

    @pl.when(first_step())
    def _():
        last_ref[...] = wide(enter)

    states = local_ref[...] + lead_ref[...] * enter
    states_ref[...] = states
    mixed_ref[...] = states * out_ref[...]
    first = sublane(states.shape) == 0
    before = jnp.where(first, last_ref[0:1, :], pltpu.roll(states, 1, 0))
    turn_ref[...] = mask_ref[...] * before - red_ref[...]
    last_ref[...] = wide(states[states.shape[0] - 1 :, :])


def cotangent_kernel(
    ids_ref, c0, c1, c2, c3, wd_ref, act_ref, we_ref,
    high_ref, low_ref, gp_ref, ge_high, ge_low, send_ref, c_sum,
    wd_high, wd_low, we_high, we_low,
):
    width = c0.shape[1]

    @pl.when(first_step())
    def _():
        split_rows(ids_ref, range(4), wd_ref, wd_high, wd_low)
        split_rows(ids_ref, (3, 1), we_ref, we_high, we_low)

    for r, c in enumerate((c0, c1, c2, c3)):
        at = slice(r * width, (r + 1) * width)
        high_ref[:, at], low_ref[:, at] = split(c[...])
        add_to(c_sum.at[:, at], row_sums(c[...]))
    grad_product = dot3((high_ref[...], low_ref[...]), (wd_high[...], wd_low[...]), NN)
    gp_ref[...] = grad_product
    ge_high[...], ge_low[...] = split(grad_product * act_ref[...])

    @apart()
    def _():
        send_ref[...] = dot3((ge_high[...], ge_low[...]), (we_high[...], we_low[...]), NT)


def back_kernel(ids_ref, ge_high, ge_low, we_ref, keep_ref, ge_sum, we_high, we_low):
    @pl.when(first_step())
    def _():
        split_rows(ids_ref, (2, 0), we_ref, we_high, we_low)

    keep_ref[...] = dot3((ge_high[...], ge_low[...]), (we_high[...], we_low[...]), NT)
    add_to(ge_sum, row_sums(ge_high[...].astype(F32) + ge_low[...].astype(F32)))


def expand_kernel(
    ids_ref, m0, m1, m2, m3, we_ref, be_ref, act_ref, slope_ref, gp_ref,
    mix_high, mix_low, prod_high, prod_low, gate_high, gate_low, gate_sum, we_high, we_low,
):
    own = m0.shape[1]

    @pl.when(first_step())
    def _():
        split_rows(ids_ref, range(4), we_ref, we_high, we_low)

    for r, m in enumerate((m0, m1, m2, m3)):
        at = slice(r * own, (r + 1) * own)
        mix_high[:, at], mix_low[:, at] = split(m[...])
    expand = dot3((mix_high[...], mix_low[...]), (we_high[...], we_low[...]), NN) + be_ref[...]
    prod_high[...], prod_low[...] = split(act_ref[...] * expand)
    grad_gate = gp_ref[...] * expand * slope_ref[...]
    gate_high[...], gate_low[...] = split(grad_gate)
    add_to(gate_sum, row_sums(grad_gate))


def output_kernel(
    ids_ref, high_ref, low_ref, wd_ref, x_ref, b_ref, far_send, far_keep, near_send, near_keep, wd_high, wd_low
):
    width = near_keep.shape[1]

    @pl.when(first_step())
    def _():
        split_rows(ids_ref, (3, 2, 1, 0), wd_ref, wd_high, wd_low)

    out = dot3((high_ref[...], low_ref[...]), (wd_high[...], wd_low[...]), NT)
    far_send[...] = out[:, :width]
    far_keep[...] = out[:, width : 2 * width]
    near_send[...] = out[:, 2 * width : 3 * width]
    near_keep[...] = out[:, 3 * width :] + x_ref[...] + b_ref[...]


def adjoint_kernel(
    keep_ref, recv_ref, far_ref, states_ref, mask_ref, out_ref, rate_ref, step_ref,
    local_ref, tail_ref, end_ref, sum_ref, carry_ref,
):
    own = far_ref.shape[1]
    log_keep = -rate_ref[...] * step_ref[...]
    keep = wide(jnp.exp(log_keep))

    @pl.when(first_step())
    def _():
        carry_ref[0:8, :] = jnp.zeros((8, 128), F32)
        carry_ref[8:16, :] = jnp.ones((8, 128), F32)

    at = sublane()
    powers = [keep, keep * keep]
    powers.append(powers[1] * powers[1])
    ramp = jnp.exp((8 - at).astype(F32) * log_keep)
    out_rate = wide(out_ref[...])
    count = far_ref.shape[0] // 8

    def step(n, carry):
        state, decay, total = carry
        here = pl.ds(pl.multiple_of((count - 1 - n) * 8, 8), 8)
        grad = keep_ref[here, own:] + recv_ref[here, own:] + far_ref[here, :]
        total = total + grad * states_ref[here, :]
        drive = grad * out_rate
        mask = mask_ref[here, :]
        value = keep * mask * drive
        for power, hop in zip(powers, (1, 2, 4)):
            inside = at < 8 - hop
            value = value + jnp.where(inside, power * mask, 0.0) * pltpu.roll(value, 8 - hop, 0)
            mask = jnp.where(inside, mask * pltpu.roll(mask, 8 - hop, 0), mask)
        factor = ramp * mask
        value = value + factor * state
        factor = factor * decay
        local_ref[here, :] = drive + jnp.where(at == 7, state, pltpu.roll(value, 7, 0))
        tail_ref[here, :] = jnp.where(at == 7, decay, pltpu.roll(factor, 7, 0))
        return (wide(value[0:1, :]), wide(factor[0:1, :]), total)

    start = (carry_ref[0:8, :], carry_ref[8:16, :], jnp.zeros((8, 128), F32))
    state, decay, total = lax.fori_loop(0, count, step, start, unroll=8)
    carry_ref[0:8, :] = state
    carry_ref[8:16, :] = decay
    end_ref[...] = jnp.where(at == 0, state, decay)
    add_to(sum_ref, total)


def add_norm_sums(ids_ref, x_ref, parts, standard_ref, sums_ref):
    width = parts[0][1].shape[1]
    standard_ref[...], _ = standardise(x_ref[...])
    for r, part in parts:
        at = pl.ds(pl.multiple_of((ids_ref[0] ^ r) * width, width), width)
        sums_ref[0:8, at] += row_sums(part * standard_ref[:, at])
        sums_ref[8:16, at] += row_sums(part)


def normed_far_kernel(
    hops, ids_ref, local_ref, tail_ref, turn_ref, slope_ref, gate_high, gate_low, x_ref,
    wg_ref, wr_ref, rate_ref, step_ref, *rest,
):
    gots = rest[:hops]
    (red_high, red_low, send_ref, keep_ref, turn_sum, red_sum, norm_sum,
     wg_high, wg_low, wr_high, wr_low, standard_ref) = rest[hops:]
    width = send_ref.shape[1]

    @pl.when(first_step())
    def _():
        split_rows(ids_ref, (3, 2), wg_ref, wg_high, wg_low)
        split_rows(ids_ref, (3, 2), wr_ref, wr_high, wr_low)
        norm_sum[...] = jnp.zeros_like(norm_sum)

    adjoint = local_ref[...] + tail_ref[...] * entering(gots)
    fresh = 1.0 - jnp.exp(-rate_ref[...] * step_ref[...])
    grad = fresh * adjoint * slope_ref[...]
    parts = split(grad)
    red_high[...], red_low[...] = parts
    add_to(turn_sum, row_sums(adjoint * turn_ref[...]))
    add_to(red_sum, row_sums(grad))
    back = dot3((gate_high[...], gate_low[...]), (wg_high[...], wg_low[...]), NT)
    back = back + dot3(parts, (wr_high[...], wr_low[...]), NT)
    send_ref[...] = back[:, :width]
    keep_ref[...] = back[:, width:]
    add_norm_sums(ids_ref, x_ref, [(3, back[:, :width]), (2, back[:, width:])], standard_ref, norm_sum)


def normed_near_kernel(
    ids_ref, red_high, red_low, gate_high, gate_low, x_ref, wg_ref, wr_ref, far_sum,
    send_ref, keep_ref, norm_ref, wg_high, wg_low, wr_high, wr_low, standard_ref, norm_sum,
):
    width = send_ref.shape[1]

    @pl.when(first_step())
    def _():
        split_rows(ids_ref, (1, 0), wg_ref, wg_high, wg_low)
        split_rows(ids_ref, (1, 0), wr_ref, wr_high, wr_low)
        norm_sum[...] = far_sum[...]

    back = dot3((gate_high[...], gate_low[...]), (wg_high[...], wg_low[...]), NT)
    back = back + dot3((red_high[...], red_low[...]), (wr_high[...], wr_low[...]), NT)
    send_ref[...] = back[:, :width]
    keep_ref[...] = back[:, width:]
    add_norm_sums(ids_ref, x_ref, [(1, back[:, :width]), (0, back[:, width:])], standard_ref, norm_sum)

    @pl.when(last_step())
    def _():
        gain = jnp.sum(norm_sum[0:8, :], axis=0, keepdims=True)
        shift = jnp.sum(norm_sum[8:16, :], axis=0, keepdims=True)
        norm_ref[...] = jnp.where(sublane(norm_ref.shape) == 0, gain, shift)


def weight_kernel(relative, ids_ref, left_high, left_low, right_high, right_low, keep_ref, send_ref, acc_ref):
    @pl.when(first_step())
    def _():
        acc_ref[...] = jnp.zeros_like(acc_ref)

    for at in range(0, acc_ref.shape[1], 256):
        to = slice(at, at + 256)
        acc_ref[:, to] += dot3((left_high[...], left_low[...]), (right_high[:, to], right_low[:, to]), TN)
    half, rows, _ = keep_ref.shape
    block = acc_ref.shape[0] // 4

    @pl.when(last_step())
    def _():
        for place in range(2 * half):
            at = ids_ref[2 + place] * rows
            if relative:
                at = ((at // block) ^ ids_ref[0]) * block + at % block
            value = acc_ref[pl.ds(pl.multiple_of(at, 8), rows), :]
            if place < half:
                keep_ref[place] = value
            else:
                send_ref[place - half] = value


def reduce_weight_kernel(
    ids_ref, left_high, left_low, right_high, right_low, vector_ref, keep_ref, send_ref, acc_ref
):
    add_to(acc_ref, dot3((left_high[...], left_low[...]), (right_high[...], right_low[...]), TN))
    half, rows, _ = keep_ref.shape
    rows = rows - 8

    @pl.when(last_step())
    def _():
        for place in range(2 * half):
            block = ids_ref[2 + place]
            to, slot = (keep_ref, place) if place < half else (send_ref, place - half)
            to[slot, :rows] = acc_ref[pl.ds(pl.multiple_of(block * rows, 8), rows), :]
            to[slot, rows:] = vector_ref[pl.ds(pl.multiple_of(block * 8, 8), 8), :]


def pack_kernel(norm_ref, down_ref, gate_ref, expand_ref, red_ref, turn_ref, out_ref,
                vector_ref, whole_ref, here_ref):
    count = vector_ref.shape[0] // 8
    vector_ref[...] = jnp.zeros_like(vector_ref)
    width = down_ref.shape[1] // 4
    here = lax.axis_index("wa")
    for r in range(4):
        at = pl.multiple_of((here ^ r) * width, width)
        here_ref[2:3, pl.ds(at, width)] = jnp.sum(down_ref[:, r * width : (r + 1) * width], axis=0, keepdims=True)
    here_ref[0:2, :] = norm_ref[0:2, :]
    rows = [here_ref[0:1, :], here_ref[1:2, :], here_ref[2:3, :]]
    rows += [jnp.sum(ref[...], axis=0, keepdims=True) for ref in (gate_ref, expand_ref, red_ref, turn_ref, out_ref)]
    for k, row in enumerate(rows):
        whole_ref[k : k + 1, : row.shape[1]] = row
    for k, row in enumerate(rows):
        size = row.shape[1] // count
        for d in range(count):
            vector_ref[d * 8 + k : d * 8 + k + 1, :size] = whole_ref[k : k + 1, d * size : (d + 1) * size]


def final_kernel(ids_ref, x_ref, gain_ref, g0, g1, g2, g3, c0, c1, c2, c3, out_ref, grad_ref, cot_ref):
    width = g0.shape[1]
    for r, (g, c) in enumerate(((g0, c0), (g1, c1), (g2, c2), (g3, c3))):
        at = pl.ds(pl.multiple_of((ids_ref[0] ^ r) * width, width), width)
        grad_ref[:, at] = g[...]
        cot_ref[:, at] = c[...]
    scale = 1.0 / x_ref.shape[1]
    standard, inv_std = standardise(x_ref[...])
    scaled = grad_ref[...] * gain_ref[...]
    first = jnp.sum(scaled, axis=1, keepdims=True) * scale
    second = jnp.sum(scaled * standard, axis=1, keepdims=True) * scale
    out_ref[...] = cot_ref[...] + inv_std * (scaled - first - standard * second)


def shape(*dims, dtype=F32):
    return jax.ShapeDtypeStruct(dims, dtype)


def tiles(array, reverse=False, column=None, tile=TILE):
    width = array.shape[1] if column is None else column

    def index(i, *ids):
        row = array.shape[0] // tile - 1 - i if reverse else i
        return (row, 0 if column is None else ids[0][0])

    return pl.BlockSpec((tile, width), index)


def fixed(array):
    return pl.BlockSpec(array.shape, lambda i, *ids: (0,) * len(array.shape))


ANYWHERE = pl.BlockSpec(memory_space=pl.ANY)


def call(us, kernel, steps, ids, ins, outs, scratch, deps=(), vmem=VMEM_LIMIT):
    in_specs = [fixed(a) if spec is None else spec for a, spec in ins] + [ANYWHERE] * len(deps)
    skip = len(ins) + (ids is not None)

    def bare(*refs):
        kernel(*refs[:skip], *refs[skip + len(deps) :])

    out_specs = [fixed(a) if spec is None else spec for a, spec in outs]
    spec = pltpu.PrefetchScalarGridSpec(
        num_scalar_prefetch=0 if ids is None else 1,
        grid=(steps,),
        in_specs=in_specs,
        out_specs=out_specs,
        scratch_shapes=[pltpu.VMEM(s, d) for s, d in scratch],
    )
    run = pl.pallas_call(
        bare,
        grid_spec=spec,
        out_shape=[a for a, _ in outs],
        compiler_params=pltpu.CompilerParams(vmem_limit_bytes=vmem),
        cost_estimate=pl.CostEstimate(flops=int(us * RATE), bytes_accessed=int(us * COST), transcendentals=0),
    )
    arrays = [a for a, _ in ins] + list(deps)
    return run(*arrays) if ids is None else run(ids, *arrays)


def after(value, *others):
    return lax.optimization_barrier((value,) + others)[0]


def wa_swap(value, distance):
    count = lax.axis_size("wa")
    return lax.ppermute(value, "wa", [(i, i ^ distance) for i in range(count)])


def seq_swap(value, distance):
    count = lax.axis_size("seq")
    return lax.ppermute(value, "seq", [(i, i ^ distance) for i in range(count)])


def seq_shift(value, hop):
    count = lax.axis_size("seq")
    pairs = [(i, i + hop) for i in range(count) if 0 <= i + hop < count]
    return lax.ppermute(value, "seq", pairs)


def block_order(bits):
    count = lax.axis_size("seq")
    if count != 8:
        return jnp.arange(count, dtype=jnp.int32)
    order = [
        sum(bit for k, bit in enumerate(bits) if place >> (2 - k) & 1) for place in range(8)
    ]
    return jnp.array(order, jnp.int32) ^ lax.axis_index("seq")


class ScatterSum:
    def __init__(self, keep, send, bits):
        self.bits = bits
        if lax.axis_size("seq") != 8:
            whole = jnp.concatenate([keep, send], axis=0)
            whole = whole.reshape(-1, whole.shape[2])
            self.total = lax.psum_scatter(whole, "seq", scatter_dimension=0, tiled=True)
            self.keep = None
            return
        self.keep = keep
        self.recv = seq_swap(send, bits[0])

    def step(self, bit, token):
        if self.keep is None:
            return token
        recv = after(self.recv, token)
        half = self.keep.shape[0] // 2
        send = self.keep[half:] + recv[half:]
        self.keep = self.keep[:half] + recv[:half]
        self.recv = seq_swap(send, bit)
        return send

    def finish(self):
        if self.keep is None:
            return self.total
        return (self.keep + self.recv)[0]


def body(
    inputs,
    seq_starts,
    ln_gain,
    ln_bias,
    w_gate,
    b_gate,
    w_reduce,
    b_reduce,
    ssm_rate,
    ssm_step,
    ssm_out,
    w_expand,
    b_expand,
    w_down,
    b_down,
    cotangent,
):
    rows, width = inputs.shape
    part = cotangent.shape[1]
    units = w_gate.shape[1]
    own = w_reduce.shape[1]
    channels = w_expand.shape[0]
    seqs = lax.axis_size("seq")
    steps = rows // TILE
    hops = min(seqs - 1, (SEQ_MAX - 2 + rows) // rows)
    here = lax.axis_index("wa").astype(jnp.int32)
    place = lax.axis_index("seq").astype(jnp.int32)

    def ids_of(bits):
        return jnp.concatenate([jnp.stack([here, place]), block_order(bits)])

    ids = ids_of((1, 2, 4))
    ids_z = ids_of((2, 1, 4))
    gain, shift, b_gate, b_red, rate, step, out_rate, b_exp, b_down_row = (
        v[None] for v in (ln_gain, ln_bias, b_gate, b_reduce, ssm_rate, ssm_step, ssm_out, b_expand, b_down)
    )
    mask = jnp.broadcast_to(1.0 - seq_starts.astype(F32)[:, None], (rows, 128))

    def t(*dims, dtype=F32):
        return shape(rows, *dims, dtype=dtype)

    def tiled(*arrays):
        return [(a, tiles(a)) for a in arrays]

    def whole(*arrays):
        return [(a, None) for a in arrays]

    cot_y = wa_swap(cotangent, 2)
    cot_c = wa_swap(cotangent, 1)

    n_high, n_low, reduced, red_slope, local, lead, end = call(
        7,
        reduce_kernel,
        steps,
        None,
        tiled(inputs) + whole(gain, shift, w_reduce, b_red, rate, step) + tiled(mask),
        tiled(t(width, dtype=BF16), t(width, dtype=BF16), t(own), t(own), t(own), t(own)) + whole(shape(8, own)),
        [((width, own), BF16)] * 2 + [((TILE, own), F32), ((16, own), F32)],
    )
    gots = [seq_shift(end, hop) for hop in range(1, hops + 1)]
    mixed, states, turn = call(
        2,
        functools.partial(states_kernel, hops),
        steps,
        None,
        tiled(local, lead, reduced, mask) + whole(out_rate, *gots),
        tiled(t(own), t(own), t(own)),
        [((8, own), F32)],
    )
    act, slope = call(
        12,
        gate_kernel,
        steps,
        None,
        tiled(n_high, n_low) + whole(w_gate, b_gate),
        tiled(t(units), t(units)),
        [((width, units), BF16)] * 2,
        [mixed],
    )
    mixed_y = wa_swap(mixed, 2)
    mixed_c = wa_swap(mixed, 1)
    cot_yc = wa_swap(after(cot_y, act), 1)
    cots = [cotangent, cot_c, cot_y, cot_yc]

    c_high, c_low, grad_product, ge_high, ge_low, back_send, c_sum = call(
        17,
        cotangent_kernel,
        steps,
        ids,
        tiled(*cots) + whole(w_down) + tiled(act) + whole(w_expand),
        tiled(
            t(width, dtype=BF16), t(width, dtype=BF16), t(units), t(units, dtype=BF16), t(units, dtype=BF16),
            t(2 * own),
        )
        + whole(shape(8, width)),
        [((width, units), BF16)] * 2 + [((2 * own, units), BF16)] * 2,
        [act],
    )
    back_recv = wa_swap(back_send, 1)
    back_keep, ge_sum = call(
        FILL,
        back_kernel,
        steps,
        ids,
        tiled(ge_high, ge_low) + whole(w_expand),
        tiled(t(2 * own)) + whole(shape(8, units)),
        [((2 * own, units), BF16)] * 2,
        [back_send],
    )
    back_far = back_keep[:, :own] + back_recv[:, :own]
    back_y = wa_swap(back_far, 2)

    mixed_yc = wa_swap(after(mixed_y, back_keep), 1)
    m_high, m_low, p_high, p_low, gg_high, gg_low, gg_sum = call(
        9,
        expand_kernel,
        steps,
        ids,
        tiled(mixed, mixed_c, mixed_y, mixed_yc) + whole(w_expand, b_exp) + tiled(act, slope, grad_product),
        tiled(
            t(channels, dtype=BF16), t(channels, dtype=BF16), t(units, dtype=BF16), t(units, dtype=BF16),
            t(units, dtype=BF16), t(units, dtype=BF16),
        )
        + whole(shape(8, units)),
        [((channels, units), BF16)] * 2,
        [back_far],
    )

    def weight(left, right, ids, relative, deps):
        blocks = left[0].shape[1] // seqs
        half = shape(seqs // 2, blocks, right[0].shape[1])
        tile = 2 * TILE
        return call(
            10,
            functools.partial(weight_kernel, relative),
            rows // tile,
            ids,
            [(a, tiles(a, tile=tile)) for a in (*left, *right)],
            whole(half, half),
            [((left[0].shape[1], right[0].shape[1]), F32)],
            deps,
        )

    w_down_keep, w_down_send = weight((c_high, c_low), (p_high, p_low), ids, True, [gg_sum])

    def backwards(*arrays):
        return [(a, tiles(a, True)) for a in arrays]

    local_back, tail, back_end, out_sum = call(
        1.5,
        adjoint_kernel,
        steps,
        None,
        backwards(back_keep, back_recv, back_y, states, mask) + whole(out_rate, rate, step),
        backwards(t(own), t(own)) + whole(shape(8, own), shape(8, own)),
        [((16, own), F32)],
        [w_down_keep],
    )
    back_gots = [seq_shift(back_end, -hop) for hop in range(1, hops + 1)]

    out_send, out_keep, near_send, near_keep = call(
        9,
        output_kernel,
        steps,
        ids,
        tiled(p_high, p_low)
        + whole(w_down)
        + [(inputs, tiles(inputs, column=part)), (b_down_row, pl.BlockSpec((1, part), lambda i, ids: (0, ids[0])))],
        tiled(t(part), t(part), t(part), t(part)),
        [((width, units), BF16)] * 2,
        [back_end],
    )
    down_sum = ScatterSum(w_down_keep, after(w_down_send, *back_gots), (1, 2, 4))
    r_high, r_low, far_send, far_keep, turn_sum, red_sum, far_norm = call(
        8,
        functools.partial(normed_far_kernel, hops),
        steps,
        ids,
        tiled(local_back, tail, turn, red_slope, gg_high, gg_low, inputs)
        + whole(w_gate, w_reduce, rate, step)
        + whole(*back_gots),
        tiled(t(own, dtype=BF16), t(own, dtype=BF16), t(part), t(part))
        + whole(shape(8, own), shape(8, own), shape(16, width)),
        [((2 * part, units), BF16)] * 2 + [((2 * part, own), BF16)] * 2 + [((TILE, width), F32)],
        [near_keep],
    )
    far_recv = wa_swap(far_send, 1)
    next_send, next_keep, norm = call(
        7,
        normed_near_kernel,
        steps,
        ids,
        tiled(r_high, r_low, gg_high, gg_low, inputs) + whole(w_gate, w_reduce, far_norm),
        tiled(t(part), t(part)) + whole(shape(8, width)),
        [((2 * part, units), BF16)] * 2
        + [((2 * part, own), BF16)] * 2
        + [((TILE, width), F32), ((16, width), F32)],
        [far_keep],
    )
    far_sum = after(far_keep, next_keep) + far_recv
    far_y = wa_swap(far_sum, 2)
    next_recv = wa_swap(next_send, 1)
    near_sum = after(next_keep, far_sum) + next_recv

    w_gate_keep, w_gate_send = weight((n_high, n_low), (gg_high, gg_low), ids_z, False, [near_sum])
    gate_total = ScatterSum(w_gate_keep, w_gate_send, (2, 1, 4))
    w_expand_keep, w_expand_send = weight((m_high, m_low), (ge_high, ge_low), ids, True, [w_gate_keep])
    expand_total = ScatterSum(w_expand_keep, w_expand_send, (1, 2, 4))
    [vector] = call(
        1.5,
        pack_kernel,
        1,
        None,
        whole(norm, c_sum, gg_sum, ge_sum, red_sum, turn_sum, out_sum),
        whole(shape(8 * seqs, 128)),
        [((8, max(width, units)), F32), ((8, width), F32)],
        [w_expand_keep],
    )
    half = shape(seqs // 2, width // seqs + 8, own)
    w_red_keep, w_red_send = call(
        5,
        reduce_weight_kernel,
        steps,
        ids,
        tiled(n_high, n_low, r_high, r_low) + whole(vector),
        whole(half, half),
        [((width, own), F32)],
        [w_expand_keep],
    )
    token = down_sum.step(2, w_red_keep)
    grad_own = after(near_sum, token) + far_y
    all_y = wa_swap(grad_own, 2)

    reduce_total = ScatterSum(w_red_keep, w_red_send, (1, 2, 4))

    out_recv = wa_swap(after(out_send, grad_own), 1)
    near_recv = wa_swap(after(near_send, grad_own), 1)
    token = gate_total.step(1, grad_own)
    token = expand_total.step(2, token)
    out_far = after(out_keep, token) + out_recv
    out_y = wa_swap(after(out_far, all_y), 2)
    near_keep = near_keep + near_recv
    token = down_sum.step(4, out_far)
    token = reduce_total.step(2, token)
    all_c = wa_swap(after(grad_own, token), 1)
    all_yc = wa_swap(after(all_y, token), 1)
    [grad_inputs] = call(
        9,
        final_kernel,
        steps,
        ids,
        tiled(inputs) + whole(gain) + tiled(grad_own, all_c, all_y, all_yc, *cots),
        tiled(t(width)),
        [((TILE, width), F32)] * 2,
        [token],
    )
    output = after(near_keep, grad_inputs) + out_y
    token = gate_total.step(4, grad_inputs)
    token = expand_total.step(4, token)
    token = reduce_total.step(4, token)

    total_w_down = down_sum.finish()
    total_w_gate = gate_total.finish()
    total_w_expand = expand_total.finish()
    total = reduce_total.finish()
    matrix_rows = width // seqs
    norm_sums = total[matrix_rows : matrix_rows + 8]
    norm_sums = norm_sums + wa_swap(norm_sums, 1)
    norm_sums = norm_sums + wa_swap(norm_sums, 2)

    def vector_of(k, length):
        return total[matrix_rows + k, : length // seqs]

    count = own // seqs
    rate_here = lax.dynamic_slice_in_dim(ssm_rate, place * count, count, 0)
    step_here = lax.dynamic_slice_in_dim(ssm_step, place * count, count, 0)
    keep_sum = vector_of(6, own)
    grad_log = -keep_sum * jnp.exp(-rate_here * step_here)
    return (
        output,
        grad_inputs,
        norm_sums[0, : width // seqs],
        norm_sums[1, : width // seqs],
        total_w_gate,
        vector_of(3, units),
        total[:matrix_rows],
        vector_of(5, own),
        grad_log * step_here,
        grad_log * rate_here,
        vector_of(7, own),
        total_w_expand,
        vector_of(4, units),
        total_w_down,
        vector_of(2, width),
    )


def solution(mesh):
    in_specs = (
        P("seq", None),
        P("seq"),
        P(),
        P(),
        P(None, "wa"),
        P("wa"),
        P(None, "wa"),
        P("wa"),
        P("wa"),
        P("wa"),
        P("wa"),
        P(None, "wa"),
        P("wa"),
        P(None, "wa"),
        P(),
        P("seq", "wa"),
    )
    out_specs = (
        P("seq", "wa"),
        P("seq", None),
        P("seq"),
        P("seq"),
        P("seq", "wa"),
        P(("wa", "seq")),
        P("seq", "wa"),
        P(("wa", "seq")),
        P(("wa", "seq")),
        P(("wa", "seq")),
        P(("wa", "seq")),
        P("seq", "wa"),
        P(("wa", "seq")),
        P("seq", "wa"),
        P("seq"),
    )
    return jax.shard_map(body, mesh=mesh, in_specs=in_specs, out_specs=out_specs, check_vma=False)
```

```python
import functools

import jax
import jax.numpy as jnp
from jax import lax
from jax.experimental import pallas as pl
from jax.experimental.pallas import tpu as pltpu
from jax.sharding import PartitionSpec as P

EPSILON = 1e-05
INV_ROOT_TAU = 0.3989422804014327
SEQ_MAX = 4096
F32 = jnp.float32
BF16 = jnp.bfloat16
VMEM_LIMIT = 20 * 2**20
TILE = 256
COST = 10**5
RATE = 5 * 10**7
FILL = 400
NN = ((1,), (0,))
NT = ((1,), (1,))
TN = ((0,), (0,))


def split(value):
    high = value.astype(BF16)
    return high, (value - high.astype(F32)).astype(BF16)


def dot(left, right, dims):
    return lax.dot_general(left, right, (dims, ((), ())), preferred_element_type=F32)


def dot3(left, right, dims):
    (left_high, left_low), (right_high, right_low) = left, right
    return dot(left_high, right_high, dims) + (
        dot(left_high, right_low, dims) + dot(left_low, right_high, dims)
    )


def gelu_parts(v):
    bell = jnp.exp(-0.5 * v * v)
    span = 1.0 + 0.23164189 * jnp.abs(v)
    t = pl.reciprocal(span, approx=True)
    t = t * (2.0 - span * t)
    tail = 0.5 * (1.061405429 * t - 1.453152027)
    tail = tail * t + 0.5 * 1.421413741
    tail = tail * t - 0.5 * 0.284496736
    tail = tail * t + 0.5 * 0.254829592
    tail = tail * t * bell
    cdf = jnp.where(v < 0.0, tail, 1.0 - tail)
    return v * cdf, cdf + (INV_ROOT_TAU * v) * bell


def standardise(values):
    scale = 1.0 / values.shape[1]
    centred = values - jnp.sum(values, axis=1, keepdims=True) * scale
    variance = jnp.sum(centred * centred, axis=1, keepdims=True) * scale
    inv_std = lax.rsqrt(variance + EPSILON)
    return centred * inv_std, inv_std


def row_sums(value):
    return jnp.sum(value.reshape(value.shape[0] // 8, 8, value.shape[1]), axis=0)


def sublane(shape=(8, 128)):
    return lax.broadcasted_iota(jnp.int32, shape, 0)


def wide(row):
    return jnp.broadcast_to(row, (8, row.shape[1]))


def entering(gots):
    total = gots[0][0:1, :]
    keep = gots[0][1:2, :]
    for got in gots[1:]:
        total = total + keep * got[0:1, :]
        keep = keep * got[1:2, :]
    return total


def first_step():
    return pl.program_id(0) == 0


def last_step():
    return pl.program_id(0) == pl.num_programs(0) - 1


def apart():
    return pl.when(pl.program_id(0) >= 0)


def add_to(ref, value):
    @pl.when(first_step())
    def _():
        ref[...] = jnp.zeros_like(ref)

    ref[...] += value


def split_rows(ids_ref, order, source_ref, high, low):
    width = high.shape[0] // len(order)
    for place, r in enumerate(order):
        at = pl.multiple_of((ids_ref[0] ^ r) * width, width)
        to = slice(place * width, (place + 1) * width)
        high[to, :], low[to, :] = split(source_ref[pl.ds(at, width), :])


def reduce_kernel(
    x_ref, gain_ref, shift_ref, w_ref, b_ref, rate_ref, step_ref, mask_ref,
    high_ref, low_ref, red_ref, slope_ref, local_ref, lead_ref, end_ref,
    w_high, w_low, drive_ref, carry_ref,
):
    log_keep = -rate_ref[...] * step_ref[...]
    keep = wide(jnp.exp(log_keep))
    fresh = 1.0 - jnp.exp(log_keep)

    @pl.when(first_step())
    def _():
        w_high[...], w_low[...] = split(w_ref[...])
        carry_ref[0:8, :] = jnp.zeros((8, 128), F32)
        carry_ref[8:16, :] = jnp.ones((8, 128), F32)

    standard, _ = standardise(x_ref[...])
    parts = split(standard * gain_ref[...] + shift_ref[...])
    high_ref[...], low_ref[...] = parts
    pre = dot3(parts, (w_high[...], w_low[...]), NN) + b_ref[...]
    reduced, slope_ref[...] = gelu_parts(pre)
    red_ref[...] = reduced
    drive_ref[...] = fresh * reduced
    at = sublane()
    powers = [keep, keep * keep]
    powers.append(powers[1] * powers[1])
    ramp = jnp.exp((at + 1).astype(F32) * log_keep)

    def step(j, carry):
        state, decay = carry
        here = pl.ds(pl.multiple_of(j * 8, 8), 8)
        value = drive_ref[here, :]
        mask = mask_ref[here, :]
        for power, hop in zip(powers, (1, 2, 4)):
            inside = at >= hop
            value = value + jnp.where(inside, power * mask, 0.0) * pltpu.roll(value, hop, 0)
            mask = jnp.where(inside, mask * pltpu.roll(mask, hop, 0), mask)
        factor = ramp * mask
        value = value + factor * state
        factor = factor * decay
        local_ref[here, :] = value
        lead_ref[here, :] = factor
        return (wide(value[7:8, :]), wide(factor[7:8, :]))

    start = (carry_ref[0:8, :], carry_ref[8:16, :])
    state, decay = lax.fori_loop(0, x_ref.shape[0] // 8, step, start, unroll=8)
    carry_ref[0:8, :] = state
    carry_ref[8:16, :] = decay
    end_ref[...] = jnp.where(at == 0, state, decay)


def gate_kernel(high_ref, low_ref, w_ref, b_ref, act_ref, slope_ref, w_high, w_low):
    @pl.when(first_step())
    def _():
        w_high[...], w_low[...] = split(w_ref[...])

    pre = dot3((high_ref[...], low_ref[...]), (w_high[...], w_low[...]), NN) + b_ref[...]
    act_ref[...], slope_ref[...] = gelu_parts(pre)


def states_kernel(hops, local_ref, lead_ref, red_ref, mask_ref, out_ref, *rest):
    gots, (mixed_ref, states_ref, turn_ref, last_ref) = rest[:hops], rest[hops:]
    enter = entering(gots)

    @pl.when(first_step())
    def _():
        last_ref[...] = wide(enter)

    states = local_ref[...] + lead_ref[...] * enter
    states_ref[...] = states
    mixed_ref[...] = states * out_ref[...]
    first = sublane(states.shape) == 0
    before = jnp.where(first, last_ref[0:1, :], pltpu.roll(states, 1, 0))
    turn_ref[...] = mask_ref[...] * before - red_ref[...]
    last_ref[...] = wide(states[states.shape[0] - 1 :, :])


def cotangent_kernel(
    ids_ref, c0, c1, c2, c3, wd_ref, act_ref, we_ref,
    high_ref, low_ref, gp_ref, ge_high, ge_low, send_ref, c_sum,
    wd_high, wd_low, we_high, we_low,
):
    width = c0.shape[1]

    @pl.when(first_step())
    def _():
        split_rows(ids_ref, range(4), wd_ref, wd_high, wd_low)
        split_rows(ids_ref, (3, 1), we_ref, we_high, we_low)

    for r, c in enumerate((c0, c1, c2, c3)):
        at = slice(r * width, (r + 1) * width)
        high_ref[:, at], low_ref[:, at] = split(c[...])
        add_to(c_sum.at[:, at], row_sums(c[...]))
    grad_product = dot3((high_ref[...], low_ref[...]), (wd_high[...], wd_low[...]), NN)
    gp_ref[...] = grad_product
    ge_high[...], ge_low[...] = split(grad_product * act_ref[...])

    @apart()
    def _():
        send_ref[...] = dot3((ge_high[...], ge_low[...]), (we_high[...], we_low[...]), NT)


def back_kernel(ids_ref, ge_high, ge_low, we_ref, keep_ref, ge_sum, we_high, we_low):
    @pl.when(first_step())
    def _():
        split_rows(ids_ref, (2, 0), we_ref, we_high, we_low)

    keep_ref[...] = dot3((ge_high[...], ge_low[...]), (we_high[...], we_low[...]), NT)
    add_to(ge_sum, row_sums(ge_high[...].astype(F32) + ge_low[...].astype(F32)))


def expand_kernel(
    ids_ref, m0, m1, m2, m3, we_ref, be_ref, act_ref, slope_ref, gp_ref,
    mix_high, mix_low, prod_high, prod_low, gate_high, gate_low, gate_sum, we_high, we_low,
):
    own = m0.shape[1]

    @pl.when(first_step())
    def _():
        split_rows(ids_ref, range(4), we_ref, we_high, we_low)

    for r, m in enumerate((m0, m1, m2, m3)):
        at = slice(r * own, (r + 1) * own)
        mix_high[:, at], mix_low[:, at] = split(m[...])
    expand = dot3((mix_high[...], mix_low[...]), (we_high[...], we_low[...]), NN) + be_ref[...]
    prod_high[...], prod_low[...] = split(act_ref[...] * expand)
    grad_gate = gp_ref[...] * expand * slope_ref[...]
    gate_high[...], gate_low[...] = split(grad_gate)
    add_to(gate_sum, row_sums(grad_gate))


def output_kernel(
    ids_ref, high_ref, low_ref, wd_ref, x_ref, b_ref, far_send, far_keep, near_send, near_keep, wd_high, wd_low
):
    width = near_keep.shape[1]

    @pl.when(first_step())
    def _():
        split_rows(ids_ref, (3, 2, 1, 0), wd_ref, wd_high, wd_low)

    out = dot3((high_ref[...], low_ref[...]), (wd_high[...], wd_low[...]), NT)
    far_send[...] = out[:, :width]
    far_keep[...] = out[:, width : 2 * width]
    near_send[...] = out[:, 2 * width : 3 * width]
    near_keep[...] = out[:, 3 * width :] + x_ref[...] + b_ref[...]


def adjoint_kernel(
    keep_ref, recv_ref, far_ref, states_ref, mask_ref, out_ref, rate_ref, step_ref,
    local_ref, tail_ref, end_ref, sum_ref, carry_ref,
):
    own = far_ref.shape[1]
    log_keep = -rate_ref[...] * step_ref[...]
    keep = wide(jnp.exp(log_keep))

    @pl.when(first_step())
    def _():
        carry_ref[0:8, :] = jnp.zeros((8, 128), F32)
        carry_ref[8:16, :] = jnp.ones((8, 128), F32)

    at = sublane()
    powers = [keep, keep * keep]
    powers.append(powers[1] * powers[1])
    ramp = jnp.exp((8 - at).astype(F32) * log_keep)
    out_rate = wide(out_ref[...])
    count = far_ref.shape[0] // 8

    def step(n, carry):
        state, decay, total = carry
        here = pl.ds(pl.multiple_of((count - 1 - n) * 8, 8), 8)
        grad = keep_ref[here, own:] + recv_ref[here, own:] + far_ref[here, :]
        total = total + grad * states_ref[here, :]
        drive = grad * out_rate
        mask = mask_ref[here, :]
        value = keep * mask * drive
        for power, hop in zip(powers, (1, 2, 4)):
            inside = at < 8 - hop
            value = value + jnp.where(inside, power * mask, 0.0) * pltpu.roll(value, 8 - hop, 0)
            mask = jnp.where(inside, mask * pltpu.roll(mask, 8 - hop, 0), mask)
        factor = ramp * mask
        value = value + factor * state
        factor = factor * decay
        local_ref[here, :] = drive + jnp.where(at == 7, state, pltpu.roll(value, 7, 0))
        tail_ref[here, :] = jnp.where(at == 7, decay, pltpu.roll(factor, 7, 0))
        return (wide(value[0:1, :]), wide(factor[0:1, :]), total)

    start = (carry_ref[0:8, :], carry_ref[8:16, :], jnp.zeros((8, 128), F32))
    state, decay, total = lax.fori_loop(0, count, step, start, unroll=8)
    carry_ref[0:8, :] = state
    carry_ref[8:16, :] = decay
    end_ref[...] = jnp.where(at == 0, state, decay)
    add_to(sum_ref, total)


def add_norm_sums(ids_ref, x_ref, parts, standard_ref, sums_ref):
    width = parts[0][1].shape[1]
    standard_ref[...], _ = standardise(x_ref[...])
    for r, part in parts:
        at = pl.ds(pl.multiple_of((ids_ref[0] ^ r) * width, width), width)
        sums_ref[0:8, at] += row_sums(part * standard_ref[:, at])
        sums_ref[8:16, at] += row_sums(part)


def normed_far_kernel(
    hops, ids_ref, local_ref, tail_ref, turn_ref, slope_ref, gate_high, gate_low, x_ref,
    wg_ref, wr_ref, rate_ref, step_ref, *rest,
):
    gots = rest[:hops]
    (red_high, red_low, send_ref, keep_ref, turn_sum, red_sum, norm_sum,
     wg_high, wg_low, wr_high, wr_low, standard_ref) = rest[hops:]
    width = send_ref.shape[1]

    @pl.when(first_step())
    def _():
        split_rows(ids_ref, (3, 2), wg_ref, wg_high, wg_low)
        split_rows(ids_ref, (3, 2), wr_ref, wr_high, wr_low)
        norm_sum[...] = jnp.zeros_like(norm_sum)

    adjoint = local_ref[...] + tail_ref[...] * entering(gots)
    fresh = 1.0 - jnp.exp(-rate_ref[...] * step_ref[...])
    grad = fresh * adjoint * slope_ref[...]
    parts = split(grad)
    red_high[...], red_low[...] = parts
    add_to(turn_sum, row_sums(adjoint * turn_ref[...]))
    add_to(red_sum, row_sums(grad))
    back = dot3((gate_high[...], gate_low[...]), (wg_high[...], wg_low[...]), NT)
    back = back + dot3(parts, (wr_high[...], wr_low[...]), NT)
    send_ref[...] = back[:, :width]
    keep_ref[...] = back[:, width:]
    add_norm_sums(ids_ref, x_ref, [(3, back[:, :width]), (2, back[:, width:])], standard_ref, norm_sum)


def normed_near_kernel(
    ids_ref, red_high, red_low, gate_high, gate_low, x_ref, wg_ref, wr_ref, far_sum,
    send_ref, keep_ref, norm_ref, wg_high, wg_low, wr_high, wr_low, standard_ref, norm_sum,
):
    width = send_ref.shape[1]

    @pl.when(first_step())
    def _():
        split_rows(ids_ref, (1, 0), wg_ref, wg_high, wg_low)
        split_rows(ids_ref, (1, 0), wr_ref, wr_high, wr_low)
        norm_sum[...] = far_sum[...]

    back = dot3((gate_high[...], gate_low[...]), (wg_high[...], wg_low[...]), NT)
    back = back + dot3((red_high[...], red_low[...]), (wr_high[...], wr_low[...]), NT)
    send_ref[...] = back[:, :width]
    keep_ref[...] = back[:, width:]
    add_norm_sums(ids_ref, x_ref, [(1, back[:, :width]), (0, back[:, width:])], standard_ref, norm_sum)

    @pl.when(last_step())
    def _():
        gain = jnp.sum(norm_sum[0:8, :], axis=0, keepdims=True)
        shift = jnp.sum(norm_sum[8:16, :], axis=0, keepdims=True)
        norm_ref[...] = jnp.where(sublane(norm_ref.shape) == 0, gain, shift)


def weight_kernel(relative, ids_ref, left_high, left_low, right_high, right_low, keep_ref, send_ref, acc_ref):
    @pl.when(first_step())
    def _():
        acc_ref[...] = jnp.zeros_like(acc_ref)

    for at in range(0, acc_ref.shape[1], 256):
        to = slice(at, at + 256)
        acc_ref[:, to] += dot3((left_high[...], left_low[...]), (right_high[:, to], right_low[:, to]), TN)
    half, rows, _ = keep_ref.shape
    block = acc_ref.shape[0] // 4

    @pl.when(last_step())
    def _():
        for place in range(2 * half):
            at = ids_ref[2 + place] * rows
            if relative:
                at = ((at // block) ^ ids_ref[0]) * block + at % block
            value = acc_ref[pl.ds(pl.multiple_of(at, 8), rows), :]
            if place < half:
                keep_ref[place] = value
            else:
                send_ref[place - half] = value


def reduce_weight_kernel(
    ids_ref, left_high, left_low, right_high, right_low, vector_ref, keep_ref, send_ref, acc_ref
):
    add_to(acc_ref, dot3((left_high[...], left_low[...]), (right_high[...], right_low[...]), TN))
    half, rows, _ = keep_ref.shape
    rows = rows - 8

    @pl.when(last_step())
    def _():
        for place in range(2 * half):
            block = ids_ref[2 + place]
            to, slot = (keep_ref, place) if place < half else (send_ref, place - half)
            to[slot, :rows] = acc_ref[pl.ds(pl.multiple_of(block * rows, 8), rows), :]
            to[slot, rows:] = vector_ref[pl.ds(pl.multiple_of(block * 8, 8), 8), :]


def pack_kernel(norm_ref, down_ref, gate_ref, expand_ref, red_ref, turn_ref, out_ref,
                vector_ref, whole_ref, here_ref):
    count = vector_ref.shape[0] // 8
    vector_ref[...] = jnp.zeros_like(vector_ref)
    width = down_ref.shape[1] // 4
    here = lax.axis_index("wa")
    for r in range(4):
        at = pl.multiple_of((here ^ r) * width, width)
        here_ref[2:3, pl.ds(at, width)] = jnp.sum(down_ref[:, r * width : (r + 1) * width], axis=0, keepdims=True)
    here_ref[0:2, :] = norm_ref[0:2, :]
    rows = [here_ref[0:1, :], here_ref[1:2, :], here_ref[2:3, :]]
    rows += [jnp.sum(ref[...], axis=0, keepdims=True) for ref in (gate_ref, expand_ref, red_ref, turn_ref, out_ref)]
    for k, row in enumerate(rows):
        whole_ref[k : k + 1, : row.shape[1]] = row
    for k, row in enumerate(rows):
        size = row.shape[1] // count
        for d in range(count):
            vector_ref[d * 8 + k : d * 8 + k + 1, :size] = whole_ref[k : k + 1, d * size : (d + 1) * size]


def final_kernel(ids_ref, x_ref, gain_ref, g0, g1, g2, g3, c0, c1, c2, c3, out_ref, grad_ref, cot_ref):
    width = g0.shape[1]
    for r, (g, c) in enumerate(((g0, c0), (g1, c1), (g2, c2), (g3, c3))):
        at = pl.ds(pl.multiple_of((ids_ref[0] ^ r) * width, width), width)
        grad_ref[:, at] = g[...]
        cot_ref[:, at] = c[...]
    scale = 1.0 / x_ref.shape[1]
    standard, inv_std = standardise(x_ref[...])
    scaled = grad_ref[...] * gain_ref[...]
    first = jnp.sum(scaled, axis=1, keepdims=True) * scale
    second = jnp.sum(scaled * standard, axis=1, keepdims=True) * scale
    out_ref[...] = cot_ref[...] + inv_std * (scaled - first - standard * second)


def shape(*dims, dtype=F32):
    return jax.ShapeDtypeStruct(dims, dtype)


def tiles(array, reverse=False, column=None, tile=TILE):
    width = array.shape[1] if column is None else column

    def index(i, *ids):
        row = array.shape[0] // tile - 1 - i if reverse else i
        return (row, 0 if column is None else ids[0][0])

    return pl.BlockSpec((tile, width), index)


def fixed(array):
    return pl.BlockSpec(array.shape, lambda i, *ids: (0,) * len(array.shape))


ANYWHERE = pl.BlockSpec(memory_space=pl.ANY)


def call(us, kernel, steps, ids, ins, outs, scratch, deps=(), vmem=VMEM_LIMIT):
    in_specs = [fixed(a) if spec is None else spec for a, spec in ins] + [ANYWHERE] * len(deps)
    skip = len(ins) + (ids is not None)

    def bare(*refs):
        kernel(*refs[:skip], *refs[skip + len(deps) :])

    out_specs = [fixed(a) if spec is None else spec for a, spec in outs]
    spec = pltpu.PrefetchScalarGridSpec(
        num_scalar_prefetch=0 if ids is None else 1,
        grid=(steps,),
        in_specs=in_specs,
        out_specs=out_specs,
        scratch_shapes=[pltpu.VMEM(s, d) for s, d in scratch],
    )
    run = pl.pallas_call(
        bare,
        grid_spec=spec,
        out_shape=[a for a, _ in outs],
        compiler_params=pltpu.CompilerParams(vmem_limit_bytes=vmem),
        cost_estimate=pl.CostEstimate(flops=int(us * RATE), bytes_accessed=int(us * COST), transcendentals=0),
    )
    arrays = [a for a, _ in ins] + list(deps)
    return run(*arrays) if ids is None else run(ids, *arrays)


def after(value, *others):
    return lax.optimization_barrier((value,) + others)[0]


def wa_swap(value, distance):
    count = lax.axis_size("wa")
    return lax.ppermute(value, "wa", [(i, i ^ distance) for i in range(count)])


def seq_swap(value, distance):
    count = lax.axis_size("seq")
    return lax.ppermute(value, "seq", [(i, i ^ distance) for i in range(count)])


def seq_shift(value, hop):
    count = lax.axis_size("seq")
    pairs = [(i, i + hop) for i in range(count) if 0 <= i + hop < count]
    return lax.ppermute(value, "seq", pairs)


def block_order(bits):
    count = lax.axis_size("seq")
    if count != 8:
        return jnp.arange(count, dtype=jnp.int32)
    order = [
        sum(bit for k, bit in enumerate(bits) if place >> (2 - k) & 1) for place in range(8)
    ]
    return jnp.array(order, jnp.int32) ^ lax.axis_index("seq")


class ScatterSum:
    def __init__(self, keep, send, bits):
        self.bits = bits
        if lax.axis_size("seq") != 8:
            whole = jnp.concatenate([keep, send], axis=0)
            whole = whole.reshape(-1, whole.shape[2])
            self.total = lax.psum_scatter(whole, "seq", scatter_dimension=0, tiled=True)
            self.keep = None
            return
        self.keep = keep
        self.recv = seq_swap(send, bits[0])

    def step(self, bit, token):
        if self.keep is None:
            return token
        recv = after(self.recv, token)
        half = self.keep.shape[0] // 2
        send = self.keep[half:] + recv[half:]
        self.keep = self.keep[:half] + recv[:half]
        self.recv = seq_swap(send, bit)
        return send

    def finish(self):
        if self.keep is None:
            return self.total
        return (self.keep + self.recv)[0]


def body(
    inputs,
    seq_starts,
    ln_gain,
    ln_bias,
    w_gate,
    b_gate,
    w_reduce,
    b_reduce,
    ssm_rate,
    ssm_step,
    ssm_out,
    w_expand,
    b_expand,
    w_down,
    b_down,
    cotangent,
):
    rows, width = inputs.shape
    part = cotangent.shape[1]
    units = w_gate.shape[1]
    own = w_reduce.shape[1]
    channels = w_expand.shape[0]
    seqs = lax.axis_size("seq")
    steps = rows // TILE
    hops = min(seqs - 1, (SEQ_MAX - 2 + rows) // rows)
    here = lax.axis_index("wa").astype(jnp.int32)
    place = lax.axis_index("seq").astype(jnp.int32)

    def ids_of(bits):
        return jnp.concatenate([jnp.stack([here, place]), block_order(bits)])

    ids = ids_of((1, 2, 4))
    ids_z = ids_of((2, 1, 4))
    gain, shift, b_gate, b_red, rate, step, out_rate, b_exp, b_down_row = (
        v[None] for v in (ln_gain, ln_bias, b_gate, b_reduce, ssm_rate, ssm_step, ssm_out, b_expand, b_down)
    )
    mask = jnp.broadcast_to(1.0 - seq_starts.astype(F32)[:, None], (rows, 128))

    def t(*dims, dtype=F32):
        return shape(rows, *dims, dtype=dtype)

    def tiled(*arrays):
        return [(a, tiles(a)) for a in arrays]

    def whole(*arrays):
        return [(a, None) for a in arrays]

    cot_y = wa_swap(cotangent, 2)
    cot_c = wa_swap(cotangent, 1)

    n_high, n_low, reduced, red_slope, local, lead, end = call(
        7,
        reduce_kernel,
        steps,
        None,
        tiled(inputs) + whole(gain, shift, w_reduce, b_red, rate, step) + tiled(mask),
        tiled(t(width, dtype=BF16), t(width, dtype=BF16), t(own), t(own), t(own), t(own)) + whole(shape(8, own)),
        [((width, own), BF16)] * 2 + [((TILE, own), F32), ((16, own), F32)],
    )
    gots = [seq_shift(end, hop) for hop in range(1, hops + 1)]
    mixed, states, turn = call(
        2,
        functools.partial(states_kernel, hops),
        steps,
        None,
        tiled(local, lead, reduced, mask) + whole(out_rate, *gots),
        tiled(t(own), t(own), t(own)),
        [((8, own), F32)],
    )
    act, slope = call(
        12,
        gate_kernel,
        steps,
        None,
        tiled(n_high, n_low) + whole(w_gate, b_gate),
        tiled(t(units), t(units)),
        [((width, units), BF16)] * 2,
        [mixed],
    )
    mixed_y = wa_swap(mixed, 2)
    mixed_c = wa_swap(mixed, 1)
    cot_yc = wa_swap(after(cot_y, act), 1)
    cots = [cotangent, cot_c, cot_y, cot_yc]

    c_high, c_low, grad_product, ge_high, ge_low, back_send, c_sum = call(
        17,
        cotangent_kernel,
        steps,
        ids,
        tiled(*cots) + whole(w_down) + tiled(act) + whole(w_expand),
        tiled(
            t(width, dtype=BF16), t(width, dtype=BF16), t(units), t(units, dtype=BF16), t(units, dtype=BF16),
            t(2 * own),
        )
        + whole(shape(8, width)),
        [((width, units), BF16)] * 2 + [((2 * own, units), BF16)] * 2,
        [act],
    )
    back_recv = wa_swap(back_send, 1)
    back_keep, ge_sum = call(
        FILL,
        back_kernel,
        steps,
        ids,
        tiled(ge_high, ge_low) + whole(w_expand),
        tiled(t(2 * own)) + whole(shape(8, units)),
        [((2 * own, units), BF16)] * 2,
        [back_send],
    )
    back_far = back_keep[:, :own] + back_recv[:, :own]
    back_y = wa_swap(back_far, 2)

    mixed_yc = wa_swap(after(mixed_y, back_keep), 1)
    m_high, m_low, p_high, p_low, gg_high, gg_low, gg_sum = call(
        9,
        expand_kernel,
        steps,
        ids,
        tiled(mixed, mixed_c, mixed_y, mixed_yc) + whole(w_expand, b_exp) + tiled(act, slope, grad_product),
        tiled(
            t(channels, dtype=BF16), t(channels, dtype=BF16), t(units, dtype=BF16), t(units, dtype=BF16),
            t(units, dtype=BF16), t(units, dtype=BF16),
        )
        + whole(shape(8, units)),
        [((channels, units), BF16)] * 2,
        [back_far],
    )

    def weight(left, right, ids, relative, deps):
        blocks = left[0].shape[1] // seqs
        half = shape(seqs // 2, blocks, right[0].shape[1])
        tile = 2 * TILE
        return call(
            10,
            functools.partial(weight_kernel, relative),
            rows // tile,
            ids,
            [(a, tiles(a, tile=tile)) for a in (*left, *right)],
            whole(half, half),
            [((left[0].shape[1], right[0].shape[1]), F32)],
            deps,
        )

    w_down_keep, w_down_send = weight((c_high, c_low), (p_high, p_low), ids, True, [gg_sum])

    def backwards(*arrays):
        return [(a, tiles(a, True)) for a in arrays]

    local_back, tail, back_end, out_sum = call(
        1.5,
        adjoint_kernel,
        steps,
        None,
        backwards(back_keep, back_recv, back_y, states, mask) + whole(out_rate, rate, step),
        backwards(t(own), t(own)) + whole(shape(8, own), shape(8, own)),
        [((16, own), F32)],
        [w_down_keep],
    )
    back_gots = [seq_shift(back_end, -hop) for hop in range(1, hops + 1)]

    w_gate_keep, w_gate_send = weight((n_high, n_low), (gg_high, gg_low), ids_z, False, [back_end])
    gate_total = ScatterSum(w_gate_keep, after(w_gate_send, *back_gots), (2, 1, 4))
    down_sum = ScatterSum(w_down_keep, after(w_down_send, *back_gots), (1, 2, 4))
    r_high, r_low, far_send, far_keep, turn_sum, red_sum, far_norm = call(
        8,
        functools.partial(normed_far_kernel, hops),
        steps,
        ids,
        tiled(local_back, tail, turn, red_slope, gg_high, gg_low, inputs)
        + whole(w_gate, w_reduce, rate, step)
        + whole(*back_gots),
        tiled(t(own, dtype=BF16), t(own, dtype=BF16), t(part), t(part))
        + whole(shape(8, own), shape(8, own), shape(16, width)),
        [((2 * part, units), BF16)] * 2 + [((2 * part, own), BF16)] * 2 + [((TILE, width), F32)],
        [w_gate_keep],
    )
    far_recv = wa_swap(far_send, 1)
    next_send, next_keep, norm = call(
        7,
        normed_near_kernel,
        steps,
        ids,
        tiled(r_high, r_low, gg_high, gg_low, inputs) + whole(w_gate, w_reduce, far_norm),
        tiled(t(part), t(part)) + whole(shape(8, width)),
        [((2 * part, units), BF16)] * 2
        + [((2 * part, own), BF16)] * 2
        + [((TILE, width), F32), ((16, width), F32)],
        [far_keep],
    )
    far_sum = after(far_keep, next_keep) + far_recv
    far_y = wa_swap(far_sum, 2)
    next_recv = wa_swap(next_send, 1)
    near_sum = after(next_keep, far_sum) + next_recv

    w_expand_keep, w_expand_send = weight((m_high, m_low), (ge_high, ge_low), ids, True, [near_sum])
    expand_total = ScatterSum(w_expand_keep, w_expand_send, (1, 2, 4))
    out_send, out_keep, near_send, near_keep = call(
        9,
        output_kernel,
        steps,
        ids,
        tiled(p_high, p_low)
        + whole(w_down)
        + [(inputs, tiles(inputs, column=part)), (b_down_row, pl.BlockSpec((1, part), lambda i, ids: (0, ids[0])))],
        tiled(t(part), t(part), t(part), t(part)),
        [((width, units), BF16)] * 2,
        [w_expand_keep],
    )
    [vector] = call(
        1.5,
        pack_kernel,
        1,
        None,
        whole(norm, c_sum, gg_sum, ge_sum, red_sum, turn_sum, out_sum),
        whole(shape(8 * seqs, 128)),
        [((8, max(width, units)), F32), ((8, width), F32)],
        [near_keep],
    )
    half = shape(seqs // 2, width // seqs + 8, own)
    w_red_keep, w_red_send = call(
        5,
        reduce_weight_kernel,
        steps,
        ids,
        tiled(n_high, n_low, r_high, r_low) + whole(vector),
        whole(half, half),
        [((width, own), F32)],
        [w_expand_keep],
    )
    token = down_sum.step(2, w_red_keep)
    grad_own = after(near_sum, token) + far_y
    all_y = wa_swap(grad_own, 2)

    reduce_total = ScatterSum(w_red_keep, w_red_send, (1, 2, 4))

    out_recv = wa_swap(after(out_send, grad_own), 1)
    near_recv = wa_swap(after(near_send, grad_own), 1)
    token = gate_total.step(1, grad_own)
    token = expand_total.step(2, token)
    out_far = after(out_keep, token) + out_recv
    out_y = wa_swap(after(out_far, all_y), 2)
    near_keep = near_keep + near_recv
    token = down_sum.step(4, out_far)
    token = reduce_total.step(2, token)
    all_c = wa_swap(after(grad_own, token), 1)
    all_yc = wa_swap(after(all_y, token), 1)
    [grad_inputs] = call(
        9,
        final_kernel,
        steps,
        ids,
        tiled(inputs) + whole(gain) + tiled(grad_own, all_c, all_y, all_yc, *cots),
        tiled(t(width)),
        [((TILE, width), F32)] * 2,
        [token],
    )
    output = after(near_keep, grad_inputs) + out_y
    token = gate_total.step(4, grad_inputs)
    token = expand_total.step(4, token)
    token = reduce_total.step(4, token)

    total_w_down = down_sum.finish()
    total_w_gate = gate_total.finish()
    total_w_expand = expand_total.finish()
    total = reduce_total.finish()
    matrix_rows = width // seqs
    norm_sums = total[matrix_rows : matrix_rows + 8]
    norm_sums = norm_sums + wa_swap(norm_sums, 1)
    norm_sums = norm_sums + wa_swap(norm_sums, 2)

    def vector_of(k, length):
        return total[matrix_rows + k, : length // seqs]

    count = own // seqs
    rate_here = lax.dynamic_slice_in_dim(ssm_rate, place * count, count, 0)
    step_here = lax.dynamic_slice_in_dim(ssm_step, place * count, count, 0)
    keep_sum = vector_of(6, own)
    grad_log = -keep_sum * jnp.exp(-rate_here * step_here)
    return (
        output,
        grad_inputs,
        norm_sums[0, : width // seqs],
        norm_sums[1, : width // seqs],
        total_w_gate,
        vector_of(3, units),
        total[:matrix_rows],
        vector_of(5, own),
        grad_log * step_here,
        grad_log * rate_here,
        vector_of(7, own),
        total_w_expand,
        vector_of(4, units),
        total_w_down,
        vector_of(2, width),
    )


def solution(mesh):
    in_specs = (
        P("seq", None),
        P("seq"),
        P(),
        P(),
        P(None, "wa"),
        P("wa"),
        P(None, "wa"),
        P("wa"),
        P("wa"),
        P("wa"),
        P("wa"),
        P(None, "wa"),
        P("wa"),
        P(None, "wa"),
        P(),
        P("seq", "wa"),
    )
    out_specs = (
        P("seq", "wa"),
        P("seq", None),
        P("seq"),
        P("seq"),
        P("seq", "wa"),
        P(("wa", "seq")),
        P("seq", "wa"),
        P(("wa", "seq")),
        P(("wa", "seq")),
        P(("wa", "seq")),
        P(("wa", "seq")),
        P("seq", "wa"),
        P(("wa", "seq")),
        P("seq", "wa"),
        P("seq"),
    )
    return jax.shard_map(body, mesh=mesh, in_specs=in_specs, out_specs=out_specs, check_vma=False)
```
